128 devices in a mesh: feat: 16 (over x, z), dp: 8 (over y, core).
Axes of the slice: x: 4, y: 4, z: 4, core: 2. Of those that a mesh axis runs over, the one named last changes fastest.
Arguments:
- features: bfloat16 [1024, 131072], P('feat', 'dp'), may hold values from -6 to 6
- self_weight: bfloat16 [1024, 512], P('feat'), may hold values from -0.1875 to 0.1875
- neigh_weight: bfloat16 [1024, 512], P('feat'), may hold values from -0.625 to 0.625
- head_weight: bfloat16 [512, 172], replicated, may hold values from -0.25 to 0.25
- neighbors: int32 [16384, 10], P('dp'), may hold values from 0 to 16383
- targets: int32 [16384], replicated, may hold values from 0 to 4095, as said below
- grad_logits: bfloat16 [4096, 172], P(('feat', 'dp')), may hold values from -6 to 6
Outputs:
- logits: bfloat16 [4096, 172], P(('feat', 'dp'))
- grad_self: float32 [1024, 512], P('feat')
- grad_neigh: float32 [1024, 512], P('feat')
- grad_head: float32 [512, 172], replicated
The draws below stay inside these ranges and needn't reach their ends.
Inputs may be any that keep to these rules, and one draw needn't show every extreme that they name: `targets`: batch node b lives on device b // 32 of feat+dp. In each block of 2048 entries (one sampled block) at most 32 entries name batch nodes of one device, and in every block some device gets exactly 32.
All inputs are finite; a program needn't handle non-finite values.
Results may differ from the reference program's by a relative error of at most 0.02.
Values may be sent and summed in bfloat16 or wider, within the bound.
No kernel may reach another device: no remote copies, remote signals or barrier semaphores. Data moves between devices by JAX's collectives and lax.ppermute only.
A program may use at most 128 MiB of HBM per device.

```python
import jax
import jax.numpy as jnp
from jax import lax

F = 1024
H = 512
C = 172
K2 = 10
HOP1 = 2048
HOP2 = 16384
BATCH_DEV = 32
BATCH = 4096
CAP = 32
N_DP = 8
DEVICES = 128


def draw_targets(key, part):
    key = jax.random.fold_in(key, 7)

    def one_block(block_key):
        key_special, key_ranking, key_shuffle, key_node = jax.random.split(block_key, 4)
        slot_total = DEVICES * CAP
        special = jax.random.randint(key_special, (), 0, DEVICES)
        ranking = jax.random.permutation(key_ranking, slot_total)
        owner_of = jnp.arange(slot_total) // CAP
        priority = ranking + jnp.where(owner_of == special, 0, slot_total)
        chosen = jnp.argsort(priority)[:HOP1]
        owners = jax.random.permutation(key_shuffle, owner_of[chosen])
        local_node = jax.random.randint(key_node, (HOP1,), 0, BATCH_DEV)
        return (owners * BATCH_DEV + local_node).astype(jnp.int32)
    row_keys = jax.random.split(key, N_DP)
    return jax.vmap(one_block)(row_keys).reshape(-1)


def set_ends(entries, rng, smallest, top_value):
    shape = entries.shape
    spot = [jax.random.randint(jax.random.fold_in(rng, axis), (), 0, shape[axis]) for axis in range(len(shape))]
    entries = entries.at[tuple(spot)].set(smallest)
    longest = shape.index(max(shape))
    spot[longest] = (spot[longest] + 1) % shape[longest]
    return entries.at[tuple(spot)].set(top_value)


def shard_levels(own_key, dims, pieces, low, largest):
    def one(position, parts):
        heights = jax.random.uniform(jax.random.fold_in(jax.random.fold_in(own_key, 6), position), (parts,), jnp.float32, low / len(pieces), largest / len(pieces))
        return jnp.repeat(jnp.exp(heights), dims[position] // parts).reshape((-1,) + (1,) * (len(dims) - position - 1))

    loudness = one(*pieces[0])
    for cut in pieces[1:]:
        loudness = loudness * one(*cut)
    return loudness


def bell_draw(rng, dims, width, reach, cuts=(), kind=jnp.bfloat16):
    result = jax.random.normal(rng, dims, jnp.float32) * width
    if len(cuts) > 0:
        result = shard_levels(rng, dims, cuts, -0.22, 0.18) * result
    return jnp.clip(result, min=-reach, max=reach).astype(kind)


def setup_inputs(seed: int = 0) -> dict:
    arg_keys = jax.random.split(jax.random.key(seed), 8)
    features = bell_draw(arg_keys[0], (F, HOP2 * N_DP), 1.0, 6.0, ((0, 16), (1, 8)))
    self_weight = bell_draw(arg_keys[1], (F, H), F ** -0.5, 0.1875, ((0, 16),))
    neigh_weight = bell_draw(arg_keys[2], (F, H), (F // K2) ** -0.5, 0.625, ((0, 16),))
    head_weight = bell_draw(arg_keys[3], (H, C), H ** -0.5, 0.25)
    neighbors = set_ends(jax.random.randint(arg_keys[4], (HOP1 * N_DP, K2), 0, HOP2), jax.random.fold_in(arg_keys[4], 1), 0, HOP2 - 1).astype(jnp.int32)
    targets = draw_targets(jax.random.fold_in(arg_keys[7], 71), 0)
    grad_logits = bell_draw(arg_keys[6], (BATCH, C), 1.0, 6.0, ((0, 128),))
    return {"features": features, "self_weight": self_weight, "neigh_weight": neigh_weight, "head_weight": head_weight, "neighbors": neighbors, "targets": targets, "grad_logits": grad_logits}


def block_inputs(pair):
    block_cols, block_nbrs = pair
    picked = block_cols[:, block_nbrs]
    neigh_mean = (jnp.sum(picked, axis=2, dtype=jnp.float32) / K2).astype(jnp.bfloat16)
    return block_cols[:, :HOP1], neigh_mean


def reference(features, self_weight, neigh_weight, head_weight, neighbors, targets, grad_logits):
    blocks = jnp.moveaxis(features.reshape(F, N_DP, HOP2), 1, 0)
    nbr_blocks = neighbors.reshape(N_DP, HOP1, K2)
    self_blocks, mean_blocks = lax.map(block_inputs, (blocks, nbr_blocks))
    self_cols = jnp.moveaxis(self_blocks, 0, 1).reshape(F, N_DP * HOP1)
    neigh_mean = jnp.moveaxis(mean_blocks, 0, 1).reshape(F, N_DP * HOP1)
    contract = (((0,), (0,)), ((), ()))
    pre = lax.dot_general(self_cols, self_weight, contract, preferred_element_type=jnp.float32)
    pre = pre + lax.dot_general(neigh_mean, neigh_weight, contract, preferred_element_type=jnp.float32)
    hidden = jax.nn.silu(pre).astype(jnp.bfloat16)
    summed = jax.ops.segment_sum(hidden.astype(jnp.float32), targets, num_segments=BATCH)
    tally = jax.ops.segment_sum(jnp.ones((N_DP * HOP1,), jnp.float32), targets, num_segments=BATCH)
    sample_count = jnp.maximum(tally, 1.0)[:, None]
    mean_two = summed / sample_count
    head_wide = head_weight.astype(jnp.float32)
    logits = jnp.dot(mean_two, head_wide, precision=lax.Precision.HIGHEST).astype(jnp.bfloat16)
    upstream = grad_logits.astype(jnp.float32)
    grad_head = jnp.dot(mean_two.T, upstream, precision=lax.Precision.HIGHEST)
    grad_mean = jnp.dot(grad_logits, head_weight.T, preferred_element_type=jnp.float32) / sample_count
    grad_hidden = grad_mean[targets]
    sigmoid_z = jax.nn.sigmoid(pre)
    grad_pre = (grad_hidden * sigmoid_z * (1.0 + pre * (1.0 - sigmoid_z))).astype(jnp.bfloat16)
    grad_self = jnp.dot(self_cols, grad_pre, preferred_element_type=jnp.float32)
    grad_neigh = jnp.dot(neigh_mean, grad_pre, preferred_element_type=jnp.float32)
    return logits, grad_self, grad_neigh, grad_head
```

```python
import functools

import jax
import jax.numpy as jnp
from jax import lax
from jax.experimental import pallas as pl
from jax.experimental.pallas import tpu as pltpu
from jax.sharding import PartitionSpec as P

UNROLL = 4
B16 = jnp.bfloat16
F32 = jnp.float32
I32 = jnp.int32
ROWS = (((0,), (0,)), ((), ()))
COLS = (((1,), (1,)), ((), ()))


def dot(left, right, dims=(((1,), (0,)), ((), ()))):
    return lax.dot_general(left, right, dims, preferred_element_type=F32)


def split_two(values):
    upper = values.astype(B16)
    return upper, (values - upper.astype(F32)).astype(B16)


def gather_kernel(nbr, tgt, feat, out, slot_target, owner_count, table, rows_out, cnt, *, slots, shift, unroll):
    half, n_cols = feat.shape
    hop = tgt.shape[0]
    fanout = nbr.shape[0] // hop
    chunk = 256
    eye = (
        lax.broadcasted_iota(I32, (chunk, chunk), 0) == lax.broadcasted_iota(I32, (chunk, chunk), 1)
    ).astype(F32).astype(B16)

    def turn(c, _):
        at = pl.multiple_of(c * chunk, chunk)
        piece = feat[:, pl.ds(at, chunk)]
        table[pl.ds(at, chunk), :] = dot(eye, jnp.concatenate([piece, piece], axis=0), COLS)
        return 0

    lax.fori_loop(0, n_cols // chunk, turn, 0, unroll=4)
    rows_out[...] = jnp.zeros_like(rows_out)

    def clear(i, _):
        cnt[i] = 0
        return 0

    lax.fori_loop(0, cnt.shape[0], clear, 0, unroll=8)
    own_lane = lax.broadcasted_iota(I32, (1, 2 * half), 1) < half
    scale = jnp.where(own_lane, 1.0, float(fanout))

    def one(i, _):
        target = tgt[i]
        owner = lax.shift_right_logical(target, shift)
        rank = cnt[owner]
        cnt[owner] = rank + 1
        slot = owner * slots + rank
        slot_target[slot] = target
        rows = [table[pl.ds(nbr[k * hop + i], 1), :] for k in range(fanout)]
        while len(rows) > 1:
            odd = rows[-1:] if len(rows) % 2 else []
            rows = [a + b for a, b in zip(rows[::2], rows[1::2])] + odd
        rows_out[pl.ds(slot, 1), :] = jnp.where(own_lane, table[pl.ds(i, 1), :], rows[0])
        return 0

    lax.fori_loop(0, hop, one, 0, unroll=unroll)

    def report(i, _):
        owner_count[i] = cnt[i]
        return 0

    lax.fori_loop(0, cnt.shape[0], report, 0, unroll=8)
    out[...] = (rows_out[...] / scale).astype(B16)


def layer_kernel(x, weight, gl, head_t, slot_node, count, part, part_nodes):
    n_feat, n_slots, lanes = x.shape
    nodes = gl.shape[0]
    pick_t = (lax.broadcasted_iota(I32, (nodes, n_slots), 0) == slot_node[...]).astype(F32).astype(B16)
    pre = jnp.zeros((n_slots, weight.shape[2]), F32)
    for f in range(0, n_feat, 2):
        pair = jnp.concatenate([x[f], x[f + 1]], axis=1)
        pre = pre + dot(pair, weight[f : f + 2].reshape(2 * lanes, -1))
    sig = jax.nn.sigmoid(pre)
    hidden = (pre * sig).astype(B16)
    node_sums = dot(pick_t, hidden)
    part_nodes[...] = node_sums.astype(B16)
    grad_slot = dot(dot(pick_t, gl[...], ROWS).astype(B16), head_t[...])
    wide_count = jnp.broadcast_to(count[...], (nodes, 128)).astype(B16)
    slot_count = jnp.maximum(dot(pick_t, wide_count, ROWS)[:, :1], 1.0)
    grad_pre = ((grad_slot / slot_count) * sig * (1.0 + pre * (1.0 - sig))).astype(B16)
    for f in range(n_feat):
        part[f, :lanes] = dot(x[f], grad_pre, ROWS).astype(B16)
    upper, lower = split_two(node_sums / count[...])
    head = (dot(gl[...], upper, ROWS) + dot(gl[...], lower, ROWS)).astype(B16)
    share = part.shape[1] - lanes
    for f in range(n_feat):
        part[f, lanes:] = head[f * share : (f + 1) * share]


def local(features, self_weight, neigh_weight, head_weight, neighbors, targets, grad_logits):
    n_feat = lax.axis_size("feat")
    n_dp = lax.axis_size("dp")
    devices = n_feat * n_dp
    hop, fanout = neighbors.shape
    half = features.shape[0]
    slots = 2 * hop // devices
    batch_dev, classes = grad_logits.shape
    width = self_weight.shape[1]
    dp_rank = lax.axis_index("dp")
    feat_rank = lax.axis_index("feat")
    group = n_dp * slots
    nodes = n_dp * batch_dev
    vmem = pl.BlockSpec(memory_space=pltpu.VMEM)
    smem = pl.BlockSpec(memory_space=pltpu.SMEM)

    weight = lax.all_gather(jnp.concatenate([self_weight, neigh_weight], axis=0), "feat", axis=0)
    row_grad = lax.all_gather(grad_logits, "dp", axis=0, tiled=True)

    own_targets = lax.dynamic_slice_in_dim(targets, dp_rank * hop, hop)
    out, slot_target, owner_count = pl.pallas_call(
        functools.partial(
            gather_kernel, slots=slots, shift=batch_dev.bit_length() - 1, unroll=UNROLL
        ),
        out_shape=(
            jax.ShapeDtypeStruct((devices * slots, 2 * half), B16),
            jax.ShapeDtypeStruct((devices * slots,), I32),
            jax.ShapeDtypeStruct((devices,), I32),
        ),
        in_specs=[smem, smem, vmem],
        out_specs=(vmem, smem, smem),
        scratch_shapes=[
            pltpu.VMEM((features.shape[1], 2 * half), F32),
            pltpu.VMEM((devices * slots, 2 * half), F32),
            pltpu.SMEM((devices,), I32),
        ],
        compiler_params=pltpu.CompilerParams(vmem_limit_bytes=48 * 1024 * 1024),
    )(neighbors.T.reshape(-1), own_targets, features)

    x = lax.all_to_all(out.reshape(n_feat, group, 2 * half), "feat", 0, 0, tiled=True)

    head_rows = jnp.pad(head_weight.T, ((0, 256 - classes), (0, 0)))
    node_ids = feat_rank * nodes + jnp.arange(nodes, dtype=I32)
    count = jnp.sum((targets[None, :] == node_ids[:, None]).astype(F32), axis=1, keepdims=True)
    count = jnp.maximum(count, 1.0)
    rank_ok = jnp.arange(slots, dtype=I32)[None, :] < owner_count[:, None]
    slot_node = jnp.where(rank_ok.reshape(-1), slot_target, -1)
    slot_node = lax.dynamic_slice_in_dim(slot_node, feat_rank * group, group)
    slot_node = jnp.where(slot_node >= 0, slot_node - feat_rank * nodes, -1)[None, :]

    padded = 16 * n_feat * -(-classes // (16 * n_feat))
    share = padded // n_feat
    lanes = 2 * half
    part, part_nodes = pl.pallas_call(
        layer_kernel,
        out_shape=(
            jax.ShapeDtypeStruct((n_feat, lanes + share, width), B16),
            jax.ShapeDtypeStruct((nodes, width), B16),
        ),
        in_specs=[vmem] * 6,
        out_specs=(vmem, vmem),
        compiler_params=pltpu.CompilerParams(vmem_limit_bytes=48 * 1024 * 1024),
    )(x, weight, jnp.pad(row_grad, ((0, 0), (0, padded - classes))), head_rows, slot_node, count)

    summed = jnp.sum(lax.all_to_all(part, "feat", 0, 0, tiled=True).astype(F32), axis=0)
    step = 1
    while step < n_dp:
        sent = summed.astype(B16)
        other = lax.ppermute(sent, "dp", [(i, i ^ step) for i in range(n_dp)])
        summed = sent.astype(F32) + other.astype(F32)
        step *= 2
    head_share = lax.all_gather(summed[lanes:].astype(B16), "feat", axis=0, tiled=True)
    grad_head = head_share[:classes].T.astype(F32)

    node_parts = lax.all_to_all(part_nodes, "dp", 0, 0, tiled=True).reshape(n_dp, batch_dev, width)
    own_count = lax.dynamic_slice_in_dim(count, dp_rank * batch_dev, batch_dev)
    mean_two = jnp.sum(node_parts.astype(F32), axis=0) / own_count
    upper, lower = split_two(mean_two)
    logits = (dot(upper, head_weight) + dot(lower, head_weight)).astype(B16)
    return logits, summed[:half], summed[half:lanes], grad_head


def solution(mesh):
    return jax.shard_map(
        local,
        mesh=mesh,
        in_specs=(
            P("feat", "dp"),
            P("feat", None),
            P("feat", None),
            P(),
            P("dp", None),
            P(),
            P(("feat", "dp"), None),
        ),
        out_specs=(P(("feat", "dp"), None), P("feat", None), P("feat", None), P()),
        check_vma=False,
    )
```

```python
import functools

import jax
import jax.numpy as jnp
from jax import lax
from jax.experimental import pallas as pl
from jax.experimental.pallas import tpu as pltpu
from jax.sharding import PartitionSpec as P

B16 = jnp.bfloat16
F32 = jnp.float32
I32 = jnp.int32
ROWS = (((0,), (0,)), ((), ()))
COLS = (((1,), (1,)), ((), ()))
BATCHED = 16
VMEM_LIMIT = 48 * 1024 * 1024


def dot(left, right, dims=(((1,), (0,)), ((), ()))):
    return lax.dot_general(left, right, dims, preferred_element_type=F32)


def split_two(values):
    upper = values.astype(B16)
    return upper, (values - upper.astype(F32)).astype(B16)


def gather_kernel(
    first, nbr, tgt, feat, out, slot_target, owner_count, held, table, rows_out, cnt, sems, *, slots, shift
):
    half, n_cols = feat.shape
    fanout, hop = nbr.shape
    parts = sems.shape[0]
    part = n_cols // parts
    chunk = 256

    def copy(p):
        at = pl.ds(p * part, part)
        return pltpu.make_async_copy(feat.at[:, at], held.at[:, at], sems.at[p])

    for p in range(parts):
        copy(p).start()
    rows_out[...] = jnp.zeros_like(rows_out)

    def clear(i, _):
        cnt[i] = 0
        return 0

    lax.fori_loop(0, cnt.shape[0], clear, 0, unroll=8)
    eye = (
        lax.broadcasted_iota(I32, (chunk, chunk), 0) == lax.broadcasted_iota(I32, (chunk, chunk), 1)
    ).astype(F32).astype(B16)

    def turn(c, _):
        at = pl.multiple_of(c * chunk, chunk)
        piece = held[:, pl.ds(at, chunk)]
        table[pl.ds(at, chunk), :] = dot(eye, jnp.concatenate([piece, piece], axis=0), COLS)
        return 0

    steps = part // chunk
    for p in range(parts):
        copy(p).wait()
        lax.fori_loop(p * steps, (p + 1) * steps, turn, 0, unroll=8)
    own_lane = lax.broadcasted_iota(I32, (1, 2 * half), 1) < half
    start = first[0]

    def several(j, _):
        base = j * BATCHED
        places, sums = [], []
        for u in range(BATCHED):
            target = tgt[start + base + u]
            owner = lax.shift_right_logical(target, shift)
            rank = cnt[owner]
            cnt[owner] = rank + 1
            places.append((owner * slots + rank, target))
        for u in range(BATCHED):
            rows = [table[pl.ds(nbr[k, base + u], 1), :] for k in range(fanout)]
            while len(rows) > 1:
                odd = rows[-1:] if len(rows) % 2 else []
                rows = [a + b for a, b in zip(rows[::2], rows[1::2])] + odd
            sums.append(jnp.where(own_lane, table[pl.ds(base + u, 1), :], rows[0]))
        for (place, target), row in zip(places, sums):
            rows_out[pl.ds(place, 1), :] = row
            slot_target[place] = target
        return 0

    lax.fori_loop(0, hop // BATCHED, several, 0)

    def report(i, _):
        owner_count[i] = cnt[i]
        return 0

    lax.fori_loop(0, cnt.shape[0], report, 0, unroll=8)
    out[...] = (rows_out[...] / jnp.where(own_lane, 1.0, float(fanout))).astype(B16)


def forward_kernel(x, weight, gl, head, head_t, slot_node, count, grad_pre, part_head, part_z):
    n_feat, n_slots, lanes = x.shape
    nodes = gl.shape[0]
    pick_t = (lax.broadcasted_iota(I32, (nodes, n_slots), 0) == slot_node[...]).astype(F32).astype(B16)
    pre = jnp.zeros((n_slots, weight.shape[2]), F32)
    for f in range(0, n_feat, 2):
        pair = jnp.concatenate([x[f], x[f + 1]], axis=1)
        pre = pre + dot(pair, weight[f : f + 2].reshape(2 * lanes, -1))
    sig = jax.nn.sigmoid(pre)
    hidden = (pre * sig).astype(B16)
    node_sums = dot(pick_t, hidden)
    upper, lower = split_two(node_sums / count[...])
    part_head[...] = (dot(gl[...], upper, ROWS) + dot(gl[...], lower, ROWS))[: part_head.shape[0]].astype(B16)
    z = (dot(upper, head[...]) + dot(lower, head[...])).astype(B16)
    groups, rows = part_z.shape[0], part_z.shape[1]
    for g in range(groups):
        at = 2 * rows * g
        part_z[g] = jnp.concatenate([z[at : at + rows], z[at + rows : at + 2 * rows]], axis=1)
    grad_slot = dot(dot(pick_t, gl[...], ROWS).astype(B16), head_t[...])
    wide_count = jnp.broadcast_to(count[...], (nodes, 128)).astype(B16)
    slot_count = jnp.maximum(dot(pick_t, wide_count, ROWS)[:, :1], 1.0)
    grad_pre[...] = ((grad_slot / slot_count) * sig * (1.0 + pre * (1.0 - sig))).astype(B16)


def weight_kernel(core, x, grad_pre, keep, send):
    n_feat, _, lanes = x.shape
    half = lanes // 2
    first = core[0] == 0
    for f in range(n_feat):
        both = dot(x[f], grad_pre[...], ROWS)
        keep[f] = jnp.where(first, both[:half], both[half:]).astype(B16)
        send[f] = jnp.where(first, both[half:], both[:half]).astype(B16)


def local(features, self_weight, neigh_weight, head_weight, neighbors, targets, grad_logits):
    n_feat = lax.axis_size("feat")
    n_dp = lax.axis_size("dp")
    devices = n_feat * n_dp
    hop, fanout = neighbors.shape
    half = features.shape[0]
    lanes = 2 * half
    slots = 2 * hop // devices
    batch_dev, classes = grad_logits.shape
    width = self_weight.shape[1]
    dp_rank = lax.axis_index("dp")
    feat_rank = lax.axis_index("feat")
    core = dp_rank % 2
    row = dp_rank // 2
    group = n_dp * slots
    nodes = n_dp * batch_dev
    wide = width // 2
    head_rows = 8 * n_dp * -(-classes // (8 * n_dp))
    head_share = head_rows // n_dp
    z_rows = batch_dev // 2
    vmem = pl.BlockSpec(memory_space=pltpu.VMEM)
    smem = pl.BlockSpec(memory_space=pltpu.SMEM)
    anywhere = pl.BlockSpec(memory_space=pl.ANY)
    params = pltpu.CompilerParams(vmem_limit_bytes=VMEM_LIMIT)

    def to_core(values):
        return lax.ppermute(values, "dp", [(i, i ^ 1) for i in range(n_dp)])

    def to_row(values, k):
        return lax.ppermute(values, "dp", [(i, i ^ (2 * k)) for i in range(n_dp)])

    def in_row_order(own, others):
        a = [own] + others
        a = [jnp.where(row % 2 == 1, a[i ^ 1], a[i]) for i in range(4)]
        return [jnp.where(row // 2 == 1, a[i ^ 2], a[i]) for i in range(4)]

    def in_core_order(own, other):
        return [jnp.where(core == 0, own, other), jnp.where(core == 0, other, own)]

    weight = lax.all_gather(jnp.concatenate([self_weight, neigh_weight], axis=0), "feat", axis=0)

    pair_grad = jnp.concatenate(in_core_order(grad_logits, to_core(grad_logits)), axis=0)
    row_grad = in_row_order(pair_grad, [to_row(pair_grad, k) for k in (1, 2, 3)])
    row_grad = jnp.concatenate(row_grad, axis=0)

    out, slot_target, owner_count = pl.pallas_call(
        functools.partial(gather_kernel, slots=slots, shift=batch_dev.bit_length() - 1),
        out_shape=(
            jax.ShapeDtypeStruct((devices * slots, lanes), B16),
            jax.ShapeDtypeStruct((devices * slots,), I32),
            jax.ShapeDtypeStruct((devices,), I32),
        ),
        in_specs=[smem, smem, smem, anywhere],
        out_specs=(vmem, smem, smem),
        scratch_shapes=[
            pltpu.VMEM(features.shape, B16),
            pltpu.VMEM((features.shape[1], lanes), F32),
            pltpu.VMEM((devices * slots, lanes), F32),
            pltpu.SMEM((devices,), I32),
            pltpu.SemaphoreType.DMA((4,)),
        ],
        compiler_params=params,
    )((dp_rank * hop)[None], neighbors.T, targets, features)

    x = lax.all_to_all(out.reshape(n_feat, group, lanes), "feat", 0, 0, tiled=True)

    node_ids = feat_rank * nodes + jnp.arange(nodes, dtype=I32)
    count = jnp.sum((targets[None, :] == node_ids[:, None]).astype(F32), axis=1, keepdims=True)
    count = jnp.maximum(count, 1.0)
    rank_ok = jnp.arange(slots, dtype=I32)[None, :] < owner_count[:, None]
    slot_node = jnp.where(rank_ok.reshape(-1), slot_target, -1)
    slot_node = lax.dynamic_slice_in_dim(slot_node, feat_rank * group, group)
    slot_node = jnp.where(slot_node >= 0, slot_node - feat_rank * nodes, -1)[None, :]

    room = wide - classes
    grad_pre, part_head, part_z = pl.pallas_call(
        forward_kernel,
        out_shape=(
            jax.ShapeDtypeStruct((group, width), B16),
            jax.ShapeDtypeStruct((head_rows, width), B16),
            jax.ShapeDtypeStruct((n_dp, z_rows, width), B16),
        ),
        in_specs=[vmem] * 7,
        out_specs=(vmem,) * 3,
        compiler_params=params,
    )(
        x,
        weight,
        jnp.pad(row_grad, ((0, 0), (0, room))),
        jnp.pad(head_weight, ((0, 0), (0, room))),
        jnp.pad(head_weight.T, ((0, room), (0, 0))),
        slot_node,
        count,
    )

    small = jnp.concatenate([part_head.reshape(n_dp, head_share, width), part_z], axis=1)
    small = small.reshape(n_dp // 2, 2, head_share + z_rows, width)
    own_small = lax.dynamic_index_in_dim(small, core, axis=1, keepdims=False)
    their_small = lax.dynamic_index_in_dim(small, 1 - core, axis=1, keepdims=False)
    pair_small = (own_small.astype(F32) + to_core(their_small).astype(F32)).astype(B16)

    def of_row(k):
        return lax.dynamic_index_in_dim(pair_small, row ^ k, axis=0, keepdims=False)

    arrived = [to_row(of_row(k), k).astype(F32) for k in (1, 2, 3)]
    own_small = (of_row(0).astype(F32) + arrived[0]) + (arrived[1] + arrived[2])
    z = own_small[head_share:]
    logits = jnp.concatenate([z[:, :classes], z[:, wide : wide + classes]], axis=0).astype(B16)

    keep, send = pl.pallas_call(
        weight_kernel,
        out_shape=(jax.ShapeDtypeStruct((n_feat, half, width), B16),) * 2,
        in_specs=[smem, vmem, vmem],
        out_specs=(vmem, vmem),
        compiler_params=params,
    )(core[None], x, grad_pre)

    pair_part = (keep.astype(F32) + to_core(send).astype(F32)).astype(B16)
    head_piece = jnp.broadcast_to(own_small[None, :head_share].astype(B16), (n_feat, head_share, width))
    parts = lax.all_to_all(
        jnp.concatenate([pair_part, head_piece], axis=1), "feat", 0, 0, tiled=True
    )
    summed = jnp.sum(parts.astype(F32), axis=0).astype(B16)
    arrived = [to_row(summed, k) for k in (1, 2, 3)]
    grads = [values[:half].astype(F32) for values in [summed] + arrived]
    grad = ((grads[0] + grads[1]) + (grads[2] + grads[3])).astype(B16)
    heads = in_row_order(summed[half:], [values[half:] for values in arrived])
    final = jnp.concatenate([grad] + heads, axis=0)
    grad_self, grad_neigh = in_core_order(final, to_core(final))
    heads = jnp.stack(
        [v[half:].reshape(n_dp // 2, head_share, width) for v in (grad_self, grad_neigh)], axis=1
    )
    grad_head = heads.reshape(head_rows, width)[:classes].T.astype(F32)
    return logits, grad_self[:half].astype(F32), grad_neigh[:half].astype(F32), grad_head


def solution(mesh):
    return jax.shard_map(
        local,
        mesh=mesh,
        in_specs=(
            P("feat", "dp"),
            P("feat", None),
            P("feat", None),
            P(),
            P("dp", None),
            P(),
            P(("feat", "dp"), None),
        ),
        out_specs=(P(("feat", "dp"), None), P("feat", None), P("feat", None), P()),
        check_vma=False,
    )
```

```python
import functools

import jax
import jax.numpy as jnp
from jax import lax
from jax.experimental import pallas as pl
from jax.experimental.pallas import tpu as pltpu
from jax.sharding import PartitionSpec as P

B16 = jnp.bfloat16
F32 = jnp.float32
I32 = jnp.int32
ROWS = (((0,), (0,)), ((), ()))
COLS = (((1,), (1,)), ((), ()))
BATCHED = 16
VMEM_LIMIT = 56 * 1024 * 1024


def dot(left, right, dims=(((1,), (0,)), ((), ()))):
    return lax.dot_general(left, right, dims, preferred_element_type=F32)


def split_two(values):
    upper = values.astype(B16)
    return upper, (values - upper.astype(F32)).astype(B16)


def gather_kernel(
    first, nbr, tgt, feat, out, slot_target, low_count, high_count,
    held, table, rows_out, ids, own_tgt, place, feat_sems, nbr_sems, tgt_sem, *, slots, shift,
):
    half, n_cols = feat.shape
    fanout, hop = nbr.shape
    parts = feat_sems.shape[0]
    part = n_cols // parts
    chunk = 256

    def feat_copy(p):
        at = pl.ds(p * part, part)
        return pltpu.make_async_copy(feat.at[:, at], held.at[:, at], feat_sems.at[p])

    def nbr_copy(k):
        return pltpu.make_async_copy(nbr.at[k], ids.at[pl.ds(k * hop, hop)], nbr_sems.at[k])

    tgt_copy = pltpu.make_async_copy(tgt.at[pl.ds(pl.multiple_of(first[0], hop), hop)], own_tgt, tgt_sem)
    tgt_copy.start()
    for p in range(parts):
        feat_copy(p).start()
    for k in range(fanout):
        nbr_copy(k).start()

    def clear(i, _):
        low_count[i] = 0
        high_count[i] = 0
        return 0

    lax.fori_loop(0, low_count.shape[0], clear, 0, unroll=8)
    rows_out[...] = jnp.zeros_like(rows_out)
    eye = (
        lax.broadcasted_iota(I32, (chunk, chunk), 0) == lax.broadcasted_iota(I32, (chunk, chunk), 1)
    ).astype(F32).astype(B16)
    tgt_copy.wait()
    turns = n_cols // chunk
    at_once = min(8, turns // parts)
    per_turn = hop // 2 // turns

    def turn(c, _):
        for v in range(at_once):
            at = pl.multiple_of((c * at_once + v) * chunk, chunk)
            piece = held[:, pl.ds(at, chunk)]
            table[pl.ds(at, chunk), :] = dot(eye, jnp.concatenate([piece, piece], axis=0), COLS)
        for v in range(0, at_once * per_turn, 8):
            base = c * at_once * per_turn + v
            samples = [(base + u, 0) for u in range(8)] + [(base + u + hop // 2, 1) for u in range(8)]
            samples = [s for pair in zip(samples[:8], samples[8:]) for s in pair]
            aims = [own_tgt[i] for i, _ in samples]
            places = []
            for (_, high), aim in zip(samples, aims):
                owner = lax.shift_right_logical(aim, shift)
                count = high_count if high else low_count
                rank = count[owner]
                count[owner] = rank + 1
                places.append(owner * slots + (slots - 1 - rank if high else rank))
            for (i, _), spot in zip(samples, places):
                place[i] = spot
            for spot, aim in zip(places, aims):
                slot_target[spot] = aim
        return 0

    steps = turns // parts // at_once
    for p in range(parts):
        feat_copy(p).wait()
        lax.fori_loop(p * steps, (p + 1) * steps, turn, 0)
    for k in range(fanout):
        nbr_copy(k).wait()
    own_lane = lax.broadcasted_iota(I32, (1, 2 * half), 1) < half

    def several(j, _):
        base = j * BATCHED
        sums = []
        for u in range(BATCHED):
            rows = [table[pl.ds(ids[k * hop + base + u], 1), :] for k in range(fanout)]
            while len(rows) > 1:
                odd = rows[-1:] if len(rows) % 2 else []
                rows = [a + b for a, b in zip(rows[::2], rows[1::2])] + odd
            sums.append(jnp.where(own_lane, table[pl.ds(base + u, 1), :], rows[0]))
        for u in range(BATCHED):
            rows_out[pl.ds(place[base + u], 1), :] = sums[u]
        return 0

    lax.fori_loop(0, hop // BATCHED, several, 0)
    scale = jnp.where(own_lane, 1.0, 1.0 / fanout)
    n_feat, deep, lanes2 = out.shape
    lanes = lanes2 // 2
    for f in range(n_feat):
        for h in range(2):
            at = (2 * f + h) * deep
            out[f, :, h * lanes : (h + 1) * lanes] = (rows_out[at : at + deep] * scale).astype(B16)


def layer_kernel(
    core, x_hbm, self_hbm, neigh_hbm, gl, head, head_t, slot_node, count, keep, send, part_head, part_z,
    x, self_w, neigh_w, x_sems, w_sems,
):
    parts = x_sems.shape[0]
    n_feat = x.shape[0]
    each = n_feat // parts
    lanes = x.shape[2] // 2
    half = lanes // 2
    nodes = gl.shape[0]
    width = self_w.shape[2]

    def copies(p):
        at = pl.ds(p * each, each)
        return [
            pltpu.make_async_copy(x_hbm.at[at], x.at[at], x_sems.at[p]),
            pltpu.make_async_copy(self_hbm.at[at], self_w.at[at], w_sems.at[2 * p]),
            pltpu.make_async_copy(neigh_hbm.at[at], neigh_w.at[at], w_sems.at[2 * p + 1]),
        ]

    for p in range(parts):
        for one in copies(p):
            one.start()

    def rows_of(f):
        both = x[f]
        return jnp.concatenate([both[:, :lanes], both[:, lanes:]], axis=0)

    n_slots = 2 * x.shape[1]
    pick_t = (lax.broadcasted_iota(I32, (nodes, n_slots), 0) == slot_node[...]).astype(F32).astype(B16)
    grad_slot = dot(dot(pick_t, gl[...], ROWS).astype(B16), head_t[...])
    wide_count = jnp.broadcast_to(count[...], (nodes, 128)).astype(B16)
    slot_count = jnp.maximum(dot(pick_t, wide_count, ROWS)[:, :1], 1.0)
    grad_slot = grad_slot / slot_count
    pre = jnp.zeros((n_slots, width), F32)
    for p in range(parts):
        for one in copies(p):
            one.wait()
        for f in range(p * each, (p + 1) * each, 2):
            pair = jnp.concatenate([rows_of(f), rows_of(f + 1)], axis=1)
            rhs = jnp.concatenate([self_w[f], neigh_w[f], self_w[f + 1], neigh_w[f + 1]], axis=0)
            pre = pre + dot(pair, rhs)
    sig = jax.nn.sigmoid(pre)
    hidden = (pre * sig).astype(B16)
    node_sums = dot(pick_t, hidden)
    upper, lower = split_two(node_sums / count[...])
    part_head[...] = (dot(gl[...], upper, ROWS) + dot(gl[...], lower, ROWS))[: part_head.shape[0]].astype(B16)
    z = (dot(upper, head[...]) + dot(lower, head[...])).astype(B16)
    groups, rows = part_z.shape[0], part_z.shape[1]
    for g in range(groups):
        at = 2 * rows * g
        part_z[g] = jnp.concatenate([z[at : at + rows], z[at + rows : at + 2 * rows]], axis=1)
    grad_pre = (grad_slot * sig * (1.0 + pre * (1.0 - sig))).astype(B16)
    first = core[0] == 0
    for f in range(n_feat):
        both = dot(rows_of(f), grad_pre, ROWS)
        keep[f] = jnp.where(first, both[:half], both[half:]).astype(B16)
        send[f] = jnp.where(first, both[half:], both[:half]).astype(B16)


def local(features, self_weight, neigh_weight, head_weight, neighbors, targets, grad_logits):
    n_feat = lax.axis_size("feat")
    n_dp = lax.axis_size("dp")
    devices = n_feat * n_dp
    hop, fanout = neighbors.shape
    half = features.shape[0]
    lanes = 2 * half
    slots = 2 * hop // devices
    batch_dev, classes = grad_logits.shape
    width = self_weight.shape[1]
    dp_rank = lax.axis_index("dp")
    feat_rank = lax.axis_index("feat")
    core = dp_rank % 2
    row = dp_rank // 2
    group = n_dp * slots
    nodes = n_dp * batch_dev
    wide = width // 2
    head_rows = 8 * n_dp * -(-classes // (8 * n_dp))
    head_share = head_rows // n_dp
    z_rows = batch_dev // 2
    vmem = pl.BlockSpec(memory_space=pltpu.VMEM)
    smem = pl.BlockSpec(memory_space=pltpu.SMEM)
    anywhere = pl.BlockSpec(memory_space=pl.ANY)
    params = pltpu.CompilerParams(vmem_limit_bytes=VMEM_LIMIT)

    def to_core(values):
        return lax.ppermute(values, "dp", [(i, i ^ 1) for i in range(n_dp)])

    def to_row(values, k):
        return lax.ppermute(values, "dp", [(i, i ^ (2 * k)) for i in range(n_dp)])

    def in_row_order(own, others):
        a = [own] + others
        a = [jnp.where(row % 2 == 1, a[i ^ 1], a[i]) for i in range(4)]
        return [jnp.where(row // 2 == 1, a[i ^ 2], a[i]) for i in range(4)]

    def in_core_order(own, other):
        return [jnp.where(core == 0, own, other), jnp.where(core == 0, other, own)]

    all_self, all_neigh = lax.all_gather((self_weight, neigh_weight), "feat", axis=0)

    pair_grad = jnp.concatenate(in_core_order(grad_logits, to_core(grad_logits)), axis=0)
    row_grad = in_row_order(pair_grad, [to_row(pair_grad, k) for k in (1, 2, 3)])
    row_grad = jnp.concatenate(row_grad, axis=0)

    out, slot_target, low_count, high_count = pl.pallas_call(
        functools.partial(gather_kernel, slots=slots, shift=batch_dev.bit_length() - 1),
        out_shape=(
            jax.ShapeDtypeStruct((n_feat, group // 2, 2 * lanes), B16),
            jax.ShapeDtypeStruct((devices * slots,), I32),
            jax.ShapeDtypeStruct((devices,), I32),
            jax.ShapeDtypeStruct((devices,), I32),
        ),
        in_specs=[smem, anywhere, anywhere, anywhere],
        out_specs=(vmem, smem, smem, smem),
        scratch_shapes=[
            pltpu.VMEM(features.shape, B16),
            pltpu.VMEM((features.shape[1], lanes), F32),
            pltpu.VMEM((devices * slots, lanes), F32),
            pltpu.SMEM((fanout * hop,), I32),
            pltpu.SMEM((hop,), I32),
            pltpu.SMEM((hop,), I32),
            pltpu.SemaphoreType.DMA((4,)),
            pltpu.SemaphoreType.DMA((fanout,)),
            pltpu.SemaphoreType.DMA,
        ],
        compiler_params=params,
    )((dp_rank * hop)[None], neighbors.T, targets, features)

    x = lax.all_to_all(out, "feat", 0, 0, tiled=True)

    node_ids = feat_rank * nodes + jnp.arange(nodes, dtype=I32)
    count = jnp.sum((targets[None, :] == node_ids[:, None]).astype(F32), axis=1, keepdims=True)
    count = jnp.maximum(count, 1.0)
    ranks = jnp.arange(slots, dtype=I32)[None, :]
    rank_ok = (ranks < low_count[:, None]) | (ranks >= slots - high_count[:, None])
    slot_node = jnp.where(rank_ok.reshape(-1), slot_target, -1)
    slot_node = lax.dynamic_slice_in_dim(slot_node, feat_rank * group, group)
    slot_node = jnp.where(slot_node >= 0, slot_node - feat_rank * nodes, -1)[None, :]

    room = wide - classes
    keep, send, part_head, part_z = pl.pallas_call(
        layer_kernel,
        out_shape=(
            jax.ShapeDtypeStruct((n_feat, half, width), B16),
            jax.ShapeDtypeStruct((n_feat, half, width), B16),
            jax.ShapeDtypeStruct((head_rows, width), B16),
            jax.ShapeDtypeStruct((n_dp, z_rows, width), B16),
        ),
        in_specs=[smem] + [anywhere] * 3 + [vmem] * 5,
        out_specs=(vmem,) * 4,
        scratch_shapes=[
            pltpu.VMEM(x.shape, B16),
            pltpu.VMEM(all_self.shape, B16),
            pltpu.VMEM(all_neigh.shape, B16),
            pltpu.SemaphoreType.DMA((4,)),
            pltpu.SemaphoreType.DMA((8,)),
        ],
        compiler_params=params,
    )(
        core[None],
        x,
        all_self,
        all_neigh,
        jnp.pad(row_grad, ((0, 0), (0, room))),
        jnp.pad(head_weight, ((0, 0), (0, room))),
        jnp.pad(head_weight.T, ((0, room), (0, 0))),
        slot_node,
        count,
    )

    small = jnp.concatenate([part_head.reshape(n_dp, head_share, width), part_z], axis=1)
    small = jnp.sum(lax.all_to_all(small, "dp", 0, 0, tiled=True).astype(F32), axis=0)
    z = small[head_share:]
    logits = jnp.concatenate([z[:, :classes], z[:, wide : wide + classes]], axis=0).astype(B16)

    pair_part = (keep.astype(F32) + to_core(send).astype(F32)).astype(B16)
    head_piece = jnp.broadcast_to(small[None, :head_share].astype(B16), (n_feat, head_share, width))
    parts = lax.all_to_all(
        jnp.concatenate([pair_part, head_piece], axis=1), "feat", 0, 0, tiled=True
    )
    summed = jnp.sum(parts.astype(F32), axis=0).astype(B16)
    arrived = [to_row(summed, k) for k in (1, 2, 3)]
    grads = [values[:half].astype(F32) for values in [summed] + arrived]
    grad = ((grads[0] + grads[1]) + (grads[2] + grads[3])).astype(B16)
    heads = in_row_order(summed[half:], [values[half:] for values in arrived])
    final = jnp.concatenate([grad] + heads, axis=0)
    grad_self, grad_neigh = in_core_order(final, to_core(final))
    heads = jnp.stack(
        [v[half:].reshape(n_dp // 2, head_share, width) for v in (grad_self, grad_neigh)], axis=1
    )
    grad_head = heads.reshape(head_rows, width)[:classes].T.astype(F32)
    return logits, grad_self[:half].astype(F32), grad_neigh[:half].astype(F32), grad_head


def solution(mesh):
    return jax.shard_map(
        local,
        mesh=mesh,
        in_specs=(
            P("feat", "dp"),
            P("feat", None),
            P("feat", None),
            P(),
            P("dp", None),
            P(),
            P(("feat", "dp"), None),
        ),
        out_specs=(P(("feat", "dp"), None), P("feat", None), P("feat", None), P()),
        check_vma=False,
    )
```

```python
import functools

import jax
import jax.numpy as jnp
from jax import lax
from jax.experimental import pallas as pl
from jax.experimental.pallas import tpu as pltpu
from jax.sharding import PartitionSpec as P

B16 = jnp.bfloat16
F32 = jnp.float32
I32 = jnp.int32
ROWS = (((0,), (0,)), ((), ()))
COLS = (((1,), (1,)), ((), ()))
BATCHED = 16
VMEM_LIMIT = 24 * 1024 * 1024
GATHER_VMEM = 56 * 1024 * 1024


def dot(left, right, dims=(((1,), (0,)), ((), ()))):
    return lax.dot_general(left, right, dims, preferred_element_type=F32)


def split_two(values):
    upper = values.astype(B16)
    return upper, (values - upper.astype(F32)).astype(B16)


def gather_kernel(
    first, nbr, tgt, feat, out, own_tgt, place,
    held, table, rows_out, tgt_rows, ids, spots, feat_sems, nbr_sems, tgt_sem, spot_sem, *, slots, shift,
):
    half, n_cols = feat.shape
    fanout, hop = nbr.shape
    parts = feat_sems.shape[0]
    part = n_cols // parts
    chunk = 256
    line = tgt.shape[1]

    def feat_copy(p):
        at = pl.ds(p * part, part)
        return pltpu.make_async_copy(feat.at[:, at], held.at[:, at], feat_sems.at[p])

    def nbr_copy(k):
        return pltpu.make_async_copy(nbr.at[k], ids.at[pl.ds(k * hop, hop)], nbr_sems.at[k])

    at = pl.ds(pl.multiple_of(first[0], hop // line), hop // line)
    tgt_copy = pltpu.make_async_copy(tgt.at[at], tgt_rows, tgt_sem)
    tgt_copy.start()
    for p in range(parts):
        feat_copy(p).start()
    for k in range(fanout):
        nbr_copy(k).start()
    rows_out[...] = jnp.zeros_like(rows_out)
    eye = (
        lax.broadcasted_iota(I32, (chunk, chunk), 0) == lax.broadcasted_iota(I32, (chunk, chunk), 1)
    ).astype(F32).astype(B16)
    n_owners = rows_out.shape[0] // slots
    owner_ids = lax.broadcasted_iota(I32, (n_owners, line), 0)
    sample = lax.broadcasted_iota(I32, (line, 2 * line), 0)
    other = lax.broadcasted_iota(I32, (line, 2 * line), 1)
    earlier = ((sample < other) | (other >= line)).astype(F32).astype(B16)
    tgt_copy.wait()
    before = jnp.zeros((n_owners, line), F32)
    for r in range(hop // line):
        row = tgt_rows[r : r + 1, :]
        owner = lax.shift_right_logical(row, shift)
        hit = (owner_ids == owner).astype(F32)
        counted = dot(hit.astype(B16), earlier)
        rank = jnp.sum(hit * (counted[:, :line] + before), axis=0, keepdims=True)
        before = before + counted[:, line:]
        own_tgt[:, r * line : (r + 1) * line] = row
        place[:, r * line : (r + 1) * line] = owner * slots + rank.astype(I32)
    spot_copy = pltpu.make_async_copy(place.at[0], spots, spot_sem)
    spot_copy.start()

    at_once = 8

    def turn(c, _):
        for v in range(at_once):
            at = pl.multiple_of((c * at_once + v) * chunk, chunk)
            piece = held[:, pl.ds(at, chunk)]
            table[pl.ds(at, chunk), :] = dot(eye, jnp.concatenate([piece, piece], axis=0), COLS)
        return 0

    steps = part // chunk // at_once
    for p in range(parts):
        feat_copy(p).wait()
        lax.fori_loop(p * steps, (p + 1) * steps, turn, 0)
    for k in range(fanout):
        nbr_copy(k).wait()
    spot_copy.wait()
    own_lane = lax.broadcasted_iota(I32, (1, 2 * half), 1) < half

    def several(j, _):
        base = j * BATCHED
        sums = []
        for u in range(BATCHED):
            rows = [table[pl.ds(ids[k * hop + base + u], 1), :] for k in range(fanout)]
            while len(rows) > 1:
                odd = rows[-1:] if len(rows) % 2 else []
                rows = [a + b for a, b in zip(rows[::2], rows[1::2])] + odd
            sums.append(jnp.where(own_lane, table[pl.ds(base + u, 1), :], rows[0]))
        for u in range(BATCHED):
            rows_out[pl.ds(spots[base + u], 1), :] = sums[u]
        return 0

    lax.fori_loop(0, hop // BATCHED, several, 0)
    scale = jnp.where(own_lane, 1.0, 1.0 / fanout)
    n_feat, deep, lanes2 = out.shape
    lanes = lanes2 // 2
    for f in range(n_feat):
        for h in range(2):
            at = (2 * f + h) * deep
            out[f, :, h * lanes : (h + 1) * lanes] = (rows_out[at : at + deep] * scale).astype(B16)


def layer_kernel(
    place, x, mine, theirs, gl, head, own_tgt, own_place, count, keep, send, part_head, part_z,
):
    n_feat = x.shape[0]
    lanes = x.shape[2] // 2
    half = lanes // 2
    nodes = gl.shape[0]
    width = mine.shape[2]
    first = place[0] == 0

    def weights_of(f):
        a, b = mine[f], theirs[f]
        return [jnp.where(first, a, b), jnp.where(first, b, a)]

    def rows_of(f):
        both = x[f]
        return jnp.concatenate([both[:, :lanes], both[:, lanes:]], axis=0)

    n_slots = 2 * x.shape[1]
    hop = own_tgt.shape[1]
    node_hit = lax.broadcasted_iota(I32, (nodes, hop), 0) == own_tgt[...] - place[1] * nodes
    slot_hit = lax.broadcasted_iota(I32, (n_slots, hop), 0) == own_place[...] - place[1] * n_slots
    pick_t = dot(node_hit.astype(F32).astype(B16), slot_hit.astype(F32).astype(B16), COLS).astype(B16)
    grad_slot = dot(dot(pick_t, gl[...], ROWS).astype(B16), head[...], COLS)
    wide_count = jnp.broadcast_to(count[...], (nodes, 128)).astype(B16)
    slot_count = jnp.maximum(dot(pick_t, wide_count, ROWS)[:, :1], 1.0)
    grad_slot = grad_slot / slot_count
    pre = jnp.zeros((n_slots, width), F32)
    for f in range(0, n_feat, 2):
        pair = jnp.concatenate([rows_of(f), rows_of(f + 1)], axis=1)
        rhs = jnp.concatenate(weights_of(f) + weights_of(f + 1), axis=0)
        pre = pre + dot(pair, rhs)
    sig = jax.nn.sigmoid(pre)
    hidden = (pre * sig).astype(B16)
    node_sums = dot(pick_t, hidden)
    upper, lower = split_two(node_sums / count[...])
    part_head[...] = (dot(gl[...], upper, ROWS) + dot(gl[...], lower, ROWS))[: part_head.shape[0]].astype(B16)
    z = (dot(upper, head[...]) + dot(lower, head[...])).astype(B16)
    groups, rows = part_z.shape[0], part_z.shape[1]
    for g in range(groups):
        at = 2 * rows * g
        part_z[g] = jnp.concatenate([z[at : at + rows], z[at + rows : at + 2 * rows]], axis=1)
    grad_pre = (grad_slot * sig * (1.0 + pre * (1.0 - sig))).astype(B16)
    for f in range(n_feat):
        both = dot(rows_of(f), grad_pre, ROWS)
        keep[f] = jnp.where(first, both[:half], both[half:]).astype(B16)
        send[f] = jnp.where(first, both[half:], both[:half]).astype(B16)


def local(features, self_weight, neigh_weight, head_weight, neighbors, targets, grad_logits):
    n_feat = lax.axis_size("feat")
    n_dp = lax.axis_size("dp")
    devices = n_feat * n_dp
    hop, fanout = neighbors.shape
    half = features.shape[0]
    lanes = 2 * half
    slots = 2 * hop // devices
    batch_dev, classes = grad_logits.shape
    width = self_weight.shape[1]
    dp_rank = lax.axis_index("dp")
    feat_rank = lax.axis_index("feat")
    core = dp_rank % 2
    row = dp_rank // 2
    group = n_dp * slots
    nodes = n_dp * batch_dev
    wide = width // 2
    head_rows = 8 * n_dp * -(-classes // (8 * n_dp))
    head_share = head_rows // n_dp
    z_rows = batch_dev // 2
    vmem = pl.BlockSpec(memory_space=pltpu.VMEM)
    smem = pl.BlockSpec(memory_space=pltpu.SMEM)
    anywhere = pl.BlockSpec(memory_space=pl.ANY)
    params = pltpu.CompilerParams(vmem_limit_bytes=VMEM_LIMIT)

    def to_core(values):
        return lax.ppermute(values, "dp", [(i, i ^ 1) for i in range(n_dp)])

    def to_row(values, k):
        return lax.ppermute(values, "dp", [(i, i ^ (2 * k)) for i in range(n_dp)])

    def in_row_order(own, others):
        a = [own] + others
        a = [jnp.where(row % 2 == 1, a[i ^ 1], a[i]) for i in range(4)]
        return [jnp.where(row // 2 == 1, a[i ^ 2], a[i]) for i in range(4)]

    def in_core_order(own, other):
        return [jnp.where(core == 0, own, other), jnp.where(core == 0, other, own)]

    all_feat = (n_feat, half, width)
    mine = jnp.where(core == 0, jnp.broadcast_to(self_weight, all_feat), jnp.broadcast_to(neigh_weight, all_feat))
    mine = lax.all_to_all(mine, "feat", 0, 0, tiled=True)
    theirs = to_core(mine)

    pair_grad = jnp.concatenate(in_core_order(grad_logits, to_core(grad_logits)), axis=0)
    row_grad = in_row_order(pair_grad, [to_row(pair_grad, k) for k in (1, 2, 3)])
    row_grad = jnp.concatenate(row_grad, axis=0)

    line = 128
    out, own_tgt, own_place = pl.pallas_call(
        functools.partial(gather_kernel, slots=slots, shift=batch_dev.bit_length() - 1),
        out_shape=(
            jax.ShapeDtypeStruct((n_feat, group // 2, 2 * lanes), B16),
            jax.ShapeDtypeStruct((1, hop), I32),
            jax.ShapeDtypeStruct((1, hop), I32),
        ),
        in_specs=[smem, anywhere, anywhere, anywhere],
        out_specs=(vmem, vmem, vmem),
        scratch_shapes=[
            pltpu.VMEM(features.shape, B16),
            pltpu.VMEM((features.shape[1], lanes), F32),
            pltpu.VMEM((devices * slots, lanes), F32),
            pltpu.VMEM((hop // line, line), I32),
            pltpu.SMEM((fanout * hop,), I32),
            pltpu.SMEM((hop,), I32),
            pltpu.SemaphoreType.DMA((4,)),
            pltpu.SemaphoreType.DMA((fanout,)),
            pltpu.SemaphoreType.DMA,
            pltpu.SemaphoreType.DMA,
        ],
        cost_estimate=pl.CostEstimate(flops=4 * 10**10, bytes_accessed=10**8, transcendentals=0),
        compiler_params=pltpu.CompilerParams(vmem_limit_bytes=GATHER_VMEM),
    )((dp_rank * (hop // line))[None], neighbors.T, targets.reshape(-1, line), features)

    x = lax.all_to_all(out, "feat", 0, 0, tiled=True)

    node_ids = feat_rank * nodes + jnp.arange(nodes, dtype=I32)
    all_targets, row_grad = lax.optimization_barrier((targets, row_grad))
    count = jnp.sum((all_targets[None, :] == node_ids[:, None]).astype(F32), axis=1, keepdims=True)
    count = jnp.maximum(count, 1.0)

    room = wide - classes
    keep, send, part_head, part_z = pl.pallas_call(
        layer_kernel,
        out_shape=(
            jax.ShapeDtypeStruct((n_feat, half, width), B16),
            jax.ShapeDtypeStruct((n_feat, half, width), B16),
            jax.ShapeDtypeStruct((head_rows, width), B16),
            jax.ShapeDtypeStruct((n_dp, z_rows, width), B16),
        ),
        in_specs=[smem] + [vmem] * 8,
        out_specs=(vmem,) * 4,
        compiler_params=params,
    )(
        jnp.stack([core, feat_rank]),
        x,
        mine,
        theirs,
        jnp.pad(row_grad, ((0, 0), (0, room))),
        jnp.pad(head_weight, ((0, 0), (0, room))),
        own_tgt,
        own_place,
        count,
    )

    small = jnp.concatenate([part_head.reshape(n_dp, head_share, width), part_z], axis=1)
    small = small.reshape(n_dp // 2, 2, head_share + z_rows, width)

    def for_row(k):
        return lax.dynamic_index_in_dim(small, row ^ k, axis=0, keepdims=False)

    arrived = [to_row(for_row(k), k).astype(F32) for k in (1, 2, 3)]
    small = ((for_row(0).astype(F32) + arrived[0]) + (arrived[1] + arrived[2])).astype(B16)
    own_small = lax.dynamic_index_in_dim(small, core, axis=0, keepdims=False)
    their_small = lax.dynamic_index_in_dim(small, 1 - core, axis=0, keepdims=False)
    small = own_small.astype(F32) + to_core(their_small).astype(F32)
    z = small[head_share:]
    logits = jnp.concatenate([z[:, :classes], z[:, wide : wide + classes]], axis=0).astype(B16)

    pair_part = (keep.astype(F32) + to_core(send).astype(F32)).astype(B16)
    head_piece = jnp.broadcast_to(small[None, :head_share].astype(B16), (n_feat, head_share, width))
    parts = lax.all_to_all(
        jnp.concatenate([pair_part, head_piece], axis=1), "feat", 0, 0, tiled=True
    )
    summed = jnp.sum(parts.astype(F32), axis=0).astype(B16)
    arrived = [to_row(summed, k) for k in (1, 2, 3)]
    grads = [values[:half].astype(F32) for values in [summed] + arrived]
    grad = ((grads[0] + grads[1]) + (grads[2] + grads[3])).astype(B16)
    heads = in_row_order(summed[half:], [values[half:] for values in arrived])
    final = jnp.concatenate([grad] + heads, axis=0)
    grad_self, grad_neigh = in_core_order(final, to_core(final))
    heads = jnp.stack(
        [v[half:].reshape(n_dp // 2, head_share, width) for v in (grad_self, grad_neigh)], axis=1
    )
    grad_head = heads.reshape(head_rows, width)[:classes].T.astype(F32)
    return logits, grad_self[:half].astype(F32), grad_neigh[:half].astype(F32), grad_head


def solution(mesh):
    return jax.shard_map(
        local,
        mesh=mesh,
        in_specs=(
            P("feat", "dp"),
            P("feat", None),
            P("feat", None),
            P(),
            P("dp", None),
            P(),
            P(("feat", "dp"), None),
        ),
        out_specs=(P(("feat", "dp"), None), P("feat", None), P("feat", None), P()),
        check_vma=False,
    )
```

```python
import functools

import jax
import jax.numpy as jnp
from jax import lax
from jax.experimental import pallas as pl
from jax.experimental.pallas import tpu as pltpu
from jax.sharding import PartitionSpec as P

B16 = jnp.bfloat16
F32 = jnp.float32
I32 = jnp.int32
ROWS = (((0,), (0,)), ((), ()))
COLS = (((1,), (1,)), ((), ()))
BATCHED = 16
VMEM_LIMIT = 60 * 1024 * 1024
GATHER_VMEM = 60 * 1024 * 1024


def dot(left, right, dims=(((1,), (0,)), ((), ()))):
    return lax.dot_general(left, right, dims, preferred_element_type=F32)


def split_two(values):
    upper = values.astype(B16)
    return upper, (values - upper.astype(F32)).astype(B16)


def gather_kernel(
    first, nbr, tgt, feat, out, own_tgt, place,
    held, table, rows_out, tgt_rows, ids, spots, feat_sems, nbr_sems, tgt_sem, spot_sem, *, slots, shift,
):
    half, n_cols = feat.shape
    fanout, hop = nbr.shape
    parts = feat_sems.shape[0]
    part = n_cols // parts
    chunk = 256
    line = tgt.shape[1]

    def feat_copy(p):
        at = pl.ds(p * part, part)
        return pltpu.make_async_copy(feat.at[:, at], held.at[:, at], feat_sems.at[p])

    def nbr_copy(k):
        return pltpu.make_async_copy(nbr.at[k], ids.at[pl.ds(k * hop, hop)], nbr_sems.at[k])

    at = pl.ds(pl.multiple_of(first[0], hop // line), hop // line)
    tgt_copy = pltpu.make_async_copy(tgt.at[at], tgt_rows, tgt_sem)
    tgt_copy.start()
    for p in range(parts):
        feat_copy(p).start()
    for k in range(fanout):
        nbr_copy(k).start()
    rows_out[...] = jnp.zeros_like(rows_out)
    eye = (
        lax.broadcasted_iota(I32, (chunk, chunk), 0) == lax.broadcasted_iota(I32, (chunk, chunk), 1)
    ).astype(F32).astype(B16)
    n_owners = rows_out.shape[0] // slots
    owner_ids = lax.broadcasted_iota(I32, (n_owners, line), 0)
    sample = lax.broadcasted_iota(I32, (line, 2 * line), 0)
    other = lax.broadcasted_iota(I32, (line, 2 * line), 1)
    earlier = ((sample < other) | (other >= line)).astype(F32).astype(B16)
    tgt_copy.wait()
    before = jnp.zeros((n_owners, line), F32)
    for r in range(hop // line):
        row = tgt_rows[r : r + 1, :]
        owner = lax.shift_right_logical(row, shift)
        hit = (owner_ids == owner).astype(F32)
        counted = dot(hit.astype(B16), earlier)
        rank = jnp.sum(hit * (counted[:, :line] + before), axis=0, keepdims=True)
        before = before + counted[:, line:]
        own_tgt[:, r * line : (r + 1) * line] = row
        place[:, r * line : (r + 1) * line] = owner * slots + rank.astype(I32)
    spot_copy = pltpu.make_async_copy(place.at[0], spots, spot_sem)
    spot_copy.start()

    at_once = 8

    def turn(c, _):
        for v in range(at_once):
            at = pl.multiple_of((c * at_once + v) * chunk, chunk)
            piece = held[:, pl.ds(at, chunk)]
            table[pl.ds(at, chunk), :] = dot(eye, jnp.concatenate([piece, piece], axis=0), COLS)
        return 0

    steps = part // chunk // at_once
    for p in range(parts):
        feat_copy(p).wait()
        lax.fori_loop(p * steps, (p + 1) * steps, turn, 0)
    for k in range(fanout):
        nbr_copy(k).wait()
    spot_copy.wait()
    own_lane = lax.broadcasted_iota(I32, (1, 2 * half), 1) < half

    def several(j, _):
        base = j * BATCHED
        sums = []
        for u in range(BATCHED):
            rows = [table[pl.ds(ids[k * hop + base + u], 1), :] for k in range(fanout)]
            while len(rows) > 1:
                odd = rows[-1:] if len(rows) % 2 else []
                rows = [a + b for a, b in zip(rows[::2], rows[1::2])] + odd
            sums.append(jnp.where(own_lane, table[pl.ds(base + u, 1), :], rows[0]))
        for u in range(BATCHED):
            rows_out[pl.ds(spots[base + u], 1), :] = sums[u]
        return 0

    lax.fori_loop(0, hop // BATCHED, several, 0)
    scale = jnp.where(own_lane, 1.0, 1.0 / fanout)
    n_feat, deep, lanes2 = out.shape
    lanes = lanes2 // 2
    for f in range(n_feat):
        for h in range(2):
            at = (2 * f + h) * deep
            out[f, :, h * lanes : (h + 1) * lanes] = (rows_out[at : at + deep] * scale).astype(B16)


def prepare_kernel(
    place, tgt_any, own_tgt_any, own_place_any, pair_any, from_1_any, from_2_any, from_3_any, head_any,
    pick_any, grad_any, gl_any, wide_head_any, count_any,
    tgt, own_tgt, own_place, pair_grad, from_1, from_2, from_3, head_t, pick_t, grad_slot, gl, head, count, sems,
):
    outside = [tgt_any, own_tgt_any, own_place_any, pair_any, from_1_any, from_2_any, from_3_any, head_any]
    inside = [tgt, own_tgt, own_place, pair_grad, from_1, from_2, from_3, head_t]
    arrive = [pltpu.make_async_copy(a, b, sems.at[i]) for i, (a, b) in enumerate(zip(outside, inside))]
    outside = [pick_any, grad_any, gl_any, wide_head_any, count_any]
    inside = [pick_t, grad_slot, gl, head, count]
    leave = [pltpu.make_async_copy(a, b, sems.at[len(arrive) + i]) for i, (a, b) in enumerate(zip(inside, outside))]
    for copy in arrive:
        copy.start()
    nodes = pick_t.shape[0]
    n_slots = pick_t.shape[1]
    classes, width = head_t.shape
    for copy in arrive:
        copy.wait()
    wide = gl.shape[1]
    pair = pair_grad.shape[0]
    line = tgt.shape[1]
    hop = own_tgt.shape[1]

    def ids(shape, axis):
        return lax.broadcasted_iota(I32, shape, axis)

    def ones_at(cond):
        return cond.astype(F32).astype(B16)

    digit = 16
    high, low = [], []
    for r in range(tgt.shape[0]):
        node = tgt[r : r + 1, :] - place[1] * nodes
        high.append(ones_at(ids((digit, line), 0) == lax.shift_right_arithmetic(node, 4)))
        low.append(ones_at(ids((digit, line), 0) == lax.bitwise_and(node, digit - 1)))
    table = dot(jnp.concatenate(high, axis=1), jnp.concatenate(low, axis=1), COLS)
    of_high = ones_at(ids((nodes, digit), 1) == lax.shift_right_logical(ids((nodes, digit), 0), 4))
    of_low = (ids((nodes, digit), 1) == lax.bitwise_and(ids((nodes, digit), 0), digit - 1)).astype(F32)
    per_node = jnp.sum(dot(of_high, table.astype(B16)) * of_low, axis=1, keepdims=True)
    count[...] = jnp.maximum(per_node, 1.0)
    leave[4].start()

    node_hit = ones_at(ids((nodes, hop), 0) == own_tgt[...] - place[1] * nodes)
    slot_hit = ones_at(ids((n_slots, hop), 0) == own_place[...] - place[1] * n_slots)
    picked = dot(node_hit, slot_hit, COLS).astype(B16)
    pick_t[...] = picked
    leave[0].start()

    widen = ones_at(ids((classes, wide), 0) == ids((classes, wide), 1))
    for k, piece in enumerate([pair_grad, from_1, from_2, from_3]):
        at = pl.multiple_of(lax.bitwise_xor(place[2], k) * pair, pair)
        gl[pl.ds(at, pair), :] = dot(piece[...], widen).astype(B16)
    padded = dot(widen, head_t[...], ROWS).astype(B16)
    head[...] = padded
    leave[2].start()
    leave[3].start()
    slot_grad = dot(dot(picked, gl[...], ROWS).astype(B16), padded)
    wide_count = jnp.broadcast_to(per_node, (nodes, line)).astype(B16)
    slot_count = jnp.maximum(dot(picked, wide_count, ROWS)[:, :1], 1.0)
    grad_slot[...] = slot_grad / slot_count
    leave[1].start()
    for copy in leave:
        copy.wait()


def layer_kernel(
    place, x_any, mine_any, theirs_any, pick_any, grad_any, gl_any, head_any, count_any, keep_any, send_any, small_any,
    x, mine, theirs, pick_t, grad_slot, gl, head, count, keep, send, small, big_sems, sems,
):
    parts = big_sems.shape[0]
    n_feat, deep, lanes2 = x.shape
    each = n_feat // parts
    lanes = lanes2 // 2
    width = mine.shape[2]

    def big_copies(p):
        at = pl.ds(p * each, each)
        pairs = [(x_any, x), (mine_any, mine), (theirs_any, theirs)]
        return [pltpu.make_async_copy(a.at[at], b.at[at], big_sems.at[p, i]) for i, (a, b) in enumerate(pairs)]

    for p in range(parts):
        for copy in big_copies(p):
            copy.start()
    outside = [pick_any, grad_any, gl_any, head_any, count_any]
    inside = [pick_t, grad_slot, gl, head, count]
    arrive = [pltpu.make_async_copy(a, b, sems.at[i]) for i, (a, b) in enumerate(zip(outside, inside))]
    for copy in arrive:
        copy.start()
    first = place[0] == 0

    def weights_of(f):
        a, b = mine[f], theirs[f]
        return [jnp.where(first, a, b), jnp.where(first, b, a)]

    pre = jnp.zeros((2 * deep, width), F32)
    for p in range(parts):
        for copy in big_copies(p):
            copy.wait()
        for f in range(p * each, (p + 1) * each, 2):
            pair = jnp.concatenate([rows_of(x, f), rows_of(x, f + 1)], axis=1)
            rhs = jnp.concatenate(weights_of(f) + weights_of(f + 1), axis=0)
            pre = pre + dot(pair, rhs)
    sig = jax.nn.sigmoid(pre)
    hidden = (pre * sig).astype(B16)
    for copy in arrive:
        copy.wait()
    grad_pre = (grad_slot[...] * sig * (1.0 + pre * (1.0 - sig))).astype(B16)
    node_mean = dot(pick_t[...], hidden) / count[...]
    upper, lower = split_two(node_mean)
    part_head = dot(gl[...], upper, ROWS) + dot(gl[...], lower, ROWS)
    z = dot(upper, head[...], COLS) + dot(lower, head[...], COLS)
    groups = small.shape[0]
    z_rows = z.shape[0] // groups // 2
    room = small.shape[1] - z_rows
    share = (room - 8) // 8 * 8
    for g in range(groups):
        at = 2 * z_rows * g
        small[g, :z_rows] = jnp.concatenate([z[at : at + z_rows], z[at + z_rows : at + 2 * z_rows]], axis=1).astype(B16)
        small[g, z_rows:] = part_head[g * share : g * share + room].astype(B16)
    leave = [pltpu.make_async_copy(small, small_any, sems.at[len(arrive)])]
    leave[0].start()
    half = keep.shape[1]
    for p in range(parts):
        for f in range(p * each, (p + 1) * each):
            both = dot(rows_of(x, f), grad_pre, ROWS)
            keep[f] = jnp.where(first, both[:half], both[half:]).astype(B16)
            send[f] = jnp.where(first, both[half:], both[:half]).astype(B16)
        at = pl.ds(p * each, each)
        for i, (held, result) in enumerate([(keep, keep_any), (send, send_any)]):
            leave.append(pltpu.make_async_copy(held.at[at], result.at[at], big_sems.at[p, i]))
            leave[-1].start()
    for copy in leave:
        copy.wait()


def rows_of(x, f):
    lanes = x.shape[2] // 2
    both = x[f]
    return jnp.concatenate([both[:, :lanes], both[:, lanes:]], axis=0)


def local(features, self_weight, neigh_weight, head_weight, neighbors, targets, grad_logits):
    n_feat = lax.axis_size("feat")
    n_dp = lax.axis_size("dp")
    devices = n_feat * n_dp
    hop, fanout = neighbors.shape
    half = features.shape[0]
    lanes = 2 * half
    slots = 2 * hop // devices
    batch_dev, classes = grad_logits.shape
    width = self_weight.shape[1]
    dp_rank = lax.axis_index("dp")
    feat_rank = lax.axis_index("feat")
    core = dp_rank % 2
    row = dp_rank // 2
    group = n_dp * slots
    nodes = n_dp * batch_dev
    wide = width // 2
    head_rows = 8 * n_dp * -(-classes // (8 * n_dp))
    head_share = head_rows // n_dp
    z_rows = batch_dev // 2
    vmem = pl.BlockSpec(memory_space=pltpu.VMEM)
    smem = pl.BlockSpec(memory_space=pltpu.SMEM)
    anywhere = pl.BlockSpec(memory_space=pl.ANY)
    params = pltpu.CompilerParams(vmem_limit_bytes=VMEM_LIMIT)

    def to_core(values):
        return lax.ppermute(values, "dp", [(i, i ^ 1) for i in range(n_dp)])

    def to_row(values, k):
        return lax.ppermute(values, "dp", [(i, i ^ (2 * k)) for i in range(n_dp)])

    def in_row_order(own, others):
        a = [own] + others
        a = [jnp.where(row % 2 == 1, a[i ^ 1], a[i]) for i in range(4)]
        return [jnp.where(row // 2 == 1, a[i ^ 2], a[i]) for i in range(4)]

    def in_core_order(own, other):
        return [jnp.where(core == 0, own, other), jnp.where(core == 0, other, own)]

    all_feat = (n_feat, half, width)
    mine = jnp.where(core == 0, jnp.broadcast_to(self_weight, all_feat), jnp.broadcast_to(neigh_weight, all_feat))
    mine = lax.all_to_all(mine, "feat", 0, 0, tiled=True)

    pair_grad = jnp.concatenate(in_core_order(grad_logits, to_core(grad_logits)), axis=0)
    other_grads = [to_row(pair_grad, k) for k in (1, 2, 3)]

    line = 128
    out, own_tgt, own_place = pl.pallas_call(
        functools.partial(gather_kernel, slots=slots, shift=batch_dev.bit_length() - 1),
        out_shape=(
            jax.ShapeDtypeStruct((n_feat, group // 2, 2 * lanes), B16),
            jax.ShapeDtypeStruct((1, hop), I32),
            jax.ShapeDtypeStruct((1, hop), I32),
        ),
        in_specs=[smem, anywhere, anywhere, anywhere],
        out_specs=(vmem, vmem, vmem),
        scratch_shapes=[
            pltpu.VMEM(features.shape, B16),
            pltpu.VMEM((features.shape[1], lanes), F32),
            pltpu.VMEM((devices * slots, lanes), F32),
            pltpu.VMEM((hop // line, line), I32),
            pltpu.SMEM((fanout * hop,), I32),
            pltpu.SMEM((hop,), I32),
            pltpu.SemaphoreType.DMA((4,)),
            pltpu.SemaphoreType.DMA((fanout,)),
            pltpu.SemaphoreType.DMA,
            pltpu.SemaphoreType.DMA,
        ],
        cost_estimate=pl.CostEstimate(flops=4 * 10**11, bytes_accessed=10**9, transcendentals=0),
        compiler_params=pltpu.CompilerParams(vmem_limit_bytes=GATHER_VMEM),
    )((dp_rank * (hop // line))[None], neighbors.T, targets.reshape(-1, line), features)

    x = lax.all_to_all(out, "feat", 0, 0, tiled=True)
    mine, own_tgt = lax.optimization_barrier((mine, own_tgt))
    theirs = to_core(mine)

    place = jnp.stack([core, feat_rank, row])
    room = head_share + 8
    prepared_shapes = (
        jax.ShapeDtypeStruct((nodes, group), B16),
        jax.ShapeDtypeStruct((group, width), F32),
        jax.ShapeDtypeStruct((nodes, wide), B16),
        jax.ShapeDtypeStruct((wide, width), B16),
        jax.ShapeDtypeStruct((nodes, 1), F32),
    )
    prepared_scratch = [pltpu.VMEM(v.shape, v.dtype) for v in prepared_shapes]
    prepared = pl.pallas_call(
        prepare_kernel,
        out_shape=prepared_shapes,
        in_specs=[smem] + [anywhere] * 8,
        out_specs=(anywhere,) * 5,
        scratch_shapes=[pltpu.VMEM((hop * n_dp // line, line), I32)]
        + [pltpu.VMEM((1, hop), I32)] * 2
        + [pltpu.VMEM(pair_grad.shape, B16)] * 4
        + [pltpu.VMEM((classes, width), B16)]
        + prepared_scratch
        + [pltpu.SemaphoreType.DMA((13,))],
        compiler_params=params,
    )(
        place,
        targets.reshape(-1, line),
        own_tgt,
        own_place,
        pair_grad,
        *other_grads,
        head_weight.T,
    )
    small_shape = jax.ShapeDtypeStruct((n_dp, z_rows + room, width), B16)
    part_shape = jax.ShapeDtypeStruct((n_feat, half, width), B16)
    keep, send, small = pl.pallas_call(
        layer_kernel,
        out_shape=(part_shape, part_shape, small_shape),
        in_specs=[smem] + [anywhere] * 8,
        out_specs=(anywhere,) * 3,
        scratch_shapes=[pltpu.VMEM(x.shape, B16), pltpu.VMEM(mine.shape, B16), pltpu.VMEM(theirs.shape, B16)]
        + prepared_scratch
        + [pltpu.VMEM(part_shape.shape, B16)] * 2
        + [pltpu.VMEM(small_shape.shape, B16)]
        + [pltpu.SemaphoreType.DMA((4, 3)), pltpu.SemaphoreType.DMA((6,))],
        compiler_params=params,
    )(place, x, mine, theirs, *prepared)
    pair_part = (keep.astype(F32) + to_core(send).astype(F32)).astype(B16)

    small = lax.all_to_all(small, "dp", 0, 0, tiled=True)
    small, pair_part = lax.optimization_barrier((small, pair_part))
    small = jnp.sum(small.astype(F32), axis=0)
    z = small[:z_rows]
    small = small[z_rows : z_rows + head_share]
    logits = jnp.concatenate([z[:, :classes], z[:, wide : wide + classes]], axis=0).astype(B16)

    head_piece = jnp.broadcast_to(small[None].astype(B16), (n_feat, head_share, width))
    parts = lax.all_to_all(
        jnp.concatenate([pair_part, head_piece], axis=1), "feat", 0, 0, tiled=True
    )
    summed = jnp.sum(parts.astype(F32), axis=0).astype(B16)
    arrived = [to_row(summed, k) for k in (1, 2, 3)]
    grads = [values[:half].astype(F32) for values in [summed] + arrived]
    grad = ((grads[0] + grads[1]) + (grads[2] + grads[3])).astype(B16)
    heads = in_row_order(summed[half:], [values[half:] for values in arrived])
    final = jnp.concatenate([grad] + heads, axis=0)
    grad_self, grad_neigh = in_core_order(final, to_core(final))
    heads = jnp.stack(
        [v[half:].reshape(n_dp // 2, head_share, width) for v in (grad_self, grad_neigh)], axis=1
    )
    grad_head = heads.reshape(head_rows, width)[:classes].T.astype(F32)
    return logits, grad_self[:half].astype(F32), grad_neigh[:half].astype(F32), grad_head


def solution(mesh):
    return jax.shard_map(
        local,
        mesh=mesh,
        in_specs=(
            P("feat", "dp"),
            P("feat", None),
            P("feat", None),
            P(),
            P("dp", None),
            P(),
            P(("feat", "dp"), None),
        ),
        out_specs=(P(("feat", "dp"), None), P("feat", None), P("feat", None), P()),
        check_vma=False,
    )
```

```python
import functools

import jax
import jax.numpy as jnp
from jax import lax
from jax.experimental import pallas as pl
from jax.experimental.pallas import tpu as pltpu
from jax.sharding import PartitionSpec as P

B16 = jnp.bfloat16
F32 = jnp.float32
I32 = jnp.int32
ROWS = (((0,), (0,)), ((), ()))
COLS = (((1,), (1,)), ((), ()))
BATCHED = 32
VMEM_LIMIT = 60 * 1024 * 1024
GATHER_VMEM = 60 * 1024 * 1024
WINDOW_VMEM = 63 * 1024 * 1024


def dot(left, right, dims=(((1,), (0,)), ((), ()))):
    return lax.dot_general(left, right, dims, preferred_element_type=F32)


def split_two(values):
    upper = values.astype(B16)
    return upper, (values - upper.astype(F32)).astype(B16)


def gather_kernel(
    nbr, tgt, feat, out, own_tgt, place,
    held, table, rows_out, tgt_rows, ids, spots, feat_sems, nbr_sems, tgt_sem, spot_sem, *, slots, shift,
):
    half, n_cols = feat.shape
    fanout, hop = nbr.shape
    parts = feat_sems.shape[0]
    part = n_cols // parts
    chunk = 256
    line = tgt.shape[1]

    def feat_copy(p):
        at = pl.ds(p * part, part)
        return pltpu.make_async_copy(feat.at[:, at], held.at[:, at], feat_sems.at[p])

    def nbr_copy(k):
        return pltpu.make_async_copy(nbr.at[k], ids.at[pl.ds(k * hop, hop)], nbr_sems.at[k])

    lines = hop // line
    at = pl.ds(pl.multiple_of(lax.axis_index("dp") * lines, lines), lines)
    tgt_copy = pltpu.make_async_copy(tgt.at[at], tgt_rows, tgt_sem)
    tgt_copy.start()
    for p in range(parts):
        feat_copy(p).start()
    for k in range(fanout):
        nbr_copy(k).start()
    rows_out[...] = jnp.zeros_like(rows_out)
    eye = (
        lax.broadcasted_iota(I32, (chunk, chunk), 0) == lax.broadcasted_iota(I32, (chunk, chunk), 1)
    ).astype(F32).astype(B16)
    n_owners = rows_out.shape[0] // slots
    owner_ids = lax.broadcasted_iota(I32, (n_owners, line), 0)
    sample = lax.broadcasted_iota(I32, (line, 2 * line), 0)
    other = lax.broadcasted_iota(I32, (line, 2 * line), 1)
    earlier = ((sample < other) | (other >= line)).astype(F32).astype(B16)
    tgt_copy.wait()
    before = jnp.zeros((n_owners, line), F32)
    for r in range(hop // line):
        row = tgt_rows[r : r + 1, :]
        owner = lax.shift_right_logical(row, shift)
        hit = (owner_ids == owner).astype(F32)
        counted = dot(hit.astype(B16), earlier)
        rank = jnp.sum(hit * (counted[:, :line] + before), axis=0, keepdims=True)
        before = before + counted[:, line:]
        own_tgt[:, r * line : (r + 1) * line] = row
        place[:, r * line : (r + 1) * line] = owner * slots + rank.astype(I32)
    spot_copy = pltpu.make_async_copy(place.at[0], spots, spot_sem)
    spot_copy.start()

    at_once = 8

    def turn(c, _):
        for v in range(0, at_once, 2):
            at = [pl.multiple_of((c * at_once + v + i) * chunk, chunk) for i in range(2)]
            pieces = [held[:, pl.ds(a, chunk)] for a in at]
            turned = dot(eye, jnp.concatenate([pieces[0]] * 2 + [pieces[1]] * 2, axis=0), COLS)
            for i in range(2):
                table[pl.ds(at[i], chunk), :] = turned[:, 2 * half * i : 2 * half * (i + 1)]
        return 0

    steps = part // chunk // at_once
    for p in range(parts):
        feat_copy(p).wait()
        lax.fori_loop(p * steps, (p + 1) * steps, turn, 0)
    for k in range(fanout):
        nbr_copy(k).wait()
    spot_copy.wait()
    own_lane = lax.broadcasted_iota(I32, (1, 2 * half), 1) < half

    def several(j, _):
        base = j * BATCHED
        sums = []
        for u in range(BATCHED):
            rows = [table[pl.ds(ids[k * hop + base + u], 1), :] for k in range(fanout)]
            while len(rows) > 1:
                odd = rows[-1:] if len(rows) % 2 else []
                rows = [a + b for a, b in zip(rows[::2], rows[1::2])] + odd
            sums.append(jnp.where(own_lane, table[pl.ds(base + u, 1), :], rows[0]))
        for u in range(BATCHED):
            rows_out[pl.ds(spots[base + u], 1), :] = sums[u]
        return 0

    lax.fori_loop(0, hop // BATCHED, several, 0)
    scale = jnp.where(own_lane, 1.0, 1.0 / fanout)
    n_feat, deep, lanes2 = out.shape
    lanes = lanes2 // 2
    for f in range(n_feat):
        for h in range(2):
            at = (2 * f + h) * deep
            out[f, :, h * lanes : (h + 1) * lanes] = (rows_out[at : at + deep] * scale).astype(B16)


def prepare_kernel(
    tgt_any, own_tgt_any, own_place_any, pair_any, from_1_any, from_2_any, from_3_any, head_any,
    pick_any, grad_any, gl_any, wide_head_any, count_any,
    tgt, own_tgt, own_place, pair_grad, from_1, from_2, from_3, head_t, pick_t, grad_slot, gl, head, count, sems,
):
    outside = [tgt_any, own_tgt_any, own_place_any, pair_any, from_1_any, from_2_any, from_3_any, head_any]
    inside = [tgt, own_tgt, own_place, pair_grad, from_1, from_2, from_3, head_t]
    arrive = [pltpu.make_async_copy(a, b, sems.at[i]) for i, (a, b) in enumerate(zip(outside, inside))]
    outside = [pick_any, grad_any, gl_any, wide_head_any, count_any]
    inside = [pick_t, grad_slot, gl, head, count]
    leave = [pltpu.make_async_copy(a, b, sems.at[len(arrive) + i]) for i, (a, b) in enumerate(zip(inside, outside))]
    for copy in arrive:
        copy.start()
    nodes = pick_t.shape[0]
    n_slots = pick_t.shape[1]
    classes, width = head_t.shape
    feat_rank = lax.axis_index("feat")
    for copy in arrive:
        copy.wait()
    wide = gl.shape[1]
    pair = pair_grad.shape[0]
    line = tgt.shape[1]
    hop = own_tgt.shape[1]

    def ids(shape, axis):
        return lax.broadcasted_iota(I32, shape, axis)

    def ones_at(cond):
        return cond.astype(F32).astype(B16)

    digit = 16
    high, low = [], []
    for r in range(tgt.shape[0]):
        node = tgt[r : r + 1, :] - feat_rank * nodes
        high.append(ones_at(ids((digit, line), 0) == lax.shift_right_arithmetic(node, 4)))
        low.append(ones_at(ids((digit, line), 0) == lax.bitwise_and(node, digit - 1)))
    table = dot(jnp.concatenate(high, axis=1), jnp.concatenate(low, axis=1), COLS)
    of_high = ones_at(ids((nodes, digit), 1) == lax.shift_right_logical(ids((nodes, digit), 0), 4))
    of_low = (ids((nodes, digit), 1) == lax.bitwise_and(ids((nodes, digit), 0), digit - 1)).astype(F32)
    per_node = jnp.sum(dot(of_high, table.astype(B16)) * of_low, axis=1, keepdims=True)
    count[...] = jnp.maximum(per_node, 1.0)
    leave[4].start()

    node_hit = ones_at(ids((nodes, hop), 0) == own_tgt[...] - feat_rank * nodes)
    slot_hit = ones_at(ids((n_slots, hop), 0) == own_place[...] - feat_rank * n_slots)
    picked = dot(node_hit, slot_hit, COLS).astype(B16)
    pick_t[...] = picked
    leave[0].start()

    widen = ones_at(ids((classes, wide), 0) == ids((classes, wide), 1))
    for k, piece in enumerate([pair_grad, from_1, from_2, from_3]):
        at = pl.multiple_of(lax.bitwise_xor(lax.shift_right_logical(lax.axis_index("dp"), 1), k) * pair, pair)
        gl[pl.ds(at, pair), :] = dot(piece[...], widen).astype(B16)
    padded = dot(widen, head_t[...], ROWS).astype(B16)
    head[...] = padded
    leave[2].start()
    leave[3].start()
    slot_grad = dot(dot(picked, gl[...], ROWS).astype(B16), padded)
    wide_count = jnp.broadcast_to(per_node, (nodes, line)).astype(B16)
    slot_count = jnp.maximum(dot(picked, wide_count, ROWS)[:, :1], 1.0)
    grad_slot[...] = slot_grad / slot_count
    leave[1].start()
    for copy in leave:
        copy.wait()


def layer_kernel(
    x_any, mine_any, theirs_any, pick_any, grad_any, gl_any, head_any, count_any, keep_any, send_any, small_any,
    x, mine, theirs, pick_t, grad_slot, gl, head, count, keep, send, small, big_sems, sems,
):
    parts = big_sems.shape[0]
    n_feat, deep, lanes2 = x.shape
    each = n_feat // parts
    lanes = lanes2 // 2
    width = mine.shape[2]

    def big_copies(p):
        at = pl.ds(p * each, each)
        pairs = [(x_any, x), (mine_any, mine), (theirs_any, theirs)]
        return [pltpu.make_async_copy(a.at[at], b.at[at], big_sems.at[p, i]) for i, (a, b) in enumerate(pairs)]

    for p in range(parts):
        for copy in big_copies(p):
            copy.start()
    outside = [pick_any, grad_any, gl_any, head_any, count_any]
    inside = [pick_t, grad_slot, gl, head, count]
    arrive = [pltpu.make_async_copy(a, b, sems.at[i]) for i, (a, b) in enumerate(zip(outside, inside))]
    for copy in arrive:
        copy.start()
    first = lax.bitwise_and(lax.axis_index("dp"), 1) == 0

    def weights_of(f):
        a, b = mine[f], theirs[f]
        return [jnp.where(first, a, b), jnp.where(first, b, a)]

    pre = jnp.zeros((2 * deep, width), F32)
    for p in range(parts):
        for copy in big_copies(p):
            copy.wait()
        for f in range(p * each, (p + 1) * each, 2):
            pair = jnp.concatenate([rows_of(x, f), rows_of(x, f + 1)], axis=1)
            rhs = jnp.concatenate(weights_of(f) + weights_of(f + 1), axis=0)
            pre = pre + dot(pair, rhs)
    sig = jax.nn.sigmoid(pre)
    hidden = (pre * sig).astype(B16)
    for copy in arrive:
        copy.wait()
    grad_pre = (grad_slot[...] * sig * (1.0 + pre * (1.0 - sig))).astype(B16)
    node_mean = dot(pick_t[...], hidden) / count[...]
    upper, lower = split_two(node_mean)
    part_head = dot(gl[...], upper, ROWS) + dot(gl[...], lower, ROWS)
    z = dot(upper, head[...], COLS) + dot(lower, head[...], COLS)
    groups, rows, _ = small.shape
    wide = width // 2
    for g in range(groups):
        at = 2 * rows * g
        z_part = [z[at : at + rows], z[at + rows : at + 2 * rows]]
        at = 3 * rows // 2 * g
        rest = part_head[at + rows : at + 3 * rows // 2]
        rest = jnp.concatenate([rest[:, :wide], rest[:, wide:]], axis=0)
        small[g] = jnp.concatenate(z_part + [part_head[at : at + rows], rest], axis=1).astype(B16)
    leave = [pltpu.make_async_copy(small, small_any, sems.at[len(arrive)])]
    leave[0].start()
    half = keep.shape[1]
    for p in range(parts):
        for f in range(p * each, (p + 1) * each):
            both = dot(rows_of(x, f), grad_pre, ROWS)
            keep[f] = jnp.where(first, both[:half], both[half:]).astype(B16)
            send[f] = jnp.where(first, both[half:], both[:half]).astype(B16)
        at = pl.ds(p * each, each)
        for i, (held, result) in enumerate([(keep, keep_any), (send, send_any)]):
            leave.append(pltpu.make_async_copy(held.at[at], result.at[at], big_sems.at[p, i]))
            leave[-1].start()
    for copy in leave:
        copy.wait()


def rows_of(x, f):
    lanes = x.shape[2] // 2
    both = x[f]
    return jnp.concatenate([both[:, :lanes], both[:, lanes:]], axis=0)


def local(features, self_weight, neigh_weight, head_weight, neighbors, targets, grad_logits):
    n_feat = lax.axis_size("feat")
    n_dp = lax.axis_size("dp")
    devices = n_feat * n_dp
    hop, fanout = neighbors.shape
    half = features.shape[0]
    lanes = 2 * half
    slots = 2 * hop // devices
    batch_dev, classes = grad_logits.shape
    width = self_weight.shape[1]
    dp_rank = lax.axis_index("dp")
    feat_rank = lax.axis_index("feat")
    core = dp_rank % 2
    row = dp_rank // 2
    group = n_dp * slots
    nodes = n_dp * batch_dev
    wide = width // 2
    head_rows = 8 * n_dp * -(-classes // (8 * n_dp))
    head_share = head_rows // n_dp
    z_rows = batch_dev // 2
    assert 2 * head_share == 3 * z_rows
    vmem = pl.BlockSpec(memory_space=pltpu.VMEM)
    smem = pl.BlockSpec(memory_space=pltpu.SMEM)
    anywhere = pl.BlockSpec(memory_space=pl.ANY)
    params = pltpu.CompilerParams(vmem_limit_bytes=VMEM_LIMIT)

    def to_core(values):
        return lax.ppermute(values, "dp", [(i, i ^ 1) for i in range(n_dp)])

    def to_row(values, k):
        return lax.ppermute(values, "dp", [(i, i ^ (2 * k)) for i in range(n_dp)])

    def in_row_order(own, others):
        a = [own] + others
        a = [jnp.where(row % 2 == 1, a[i ^ 1], a[i]) for i in range(4)]
        return [jnp.where(row // 2 == 1, a[i ^ 2], a[i]) for i in range(4)]

    def in_core_order(own, other):
        return [jnp.where(core == 0, own, other), jnp.where(core == 0, other, own)]

    all_feat = (n_feat, half, width)
    mine = jnp.where(core == 0, jnp.broadcast_to(self_weight, all_feat), jnp.broadcast_to(neigh_weight, all_feat))
    mine = lax.all_to_all(mine, "feat", 0, 0, tiled=True)

    pair_grad = jnp.concatenate(in_core_order(grad_logits, to_core(grad_logits)), axis=0)
    other_grads = [to_row(pair_grad, k) for k in (1, 2, 3)]

    line = 128
    out, own_tgt, own_place = pl.pallas_call(
        functools.partial(gather_kernel, slots=slots, shift=batch_dev.bit_length() - 1),
        out_shape=(
            jax.ShapeDtypeStruct((n_feat, group // 2, 2 * lanes), B16),
            jax.ShapeDtypeStruct((1, hop), I32),
            jax.ShapeDtypeStruct((1, hop), I32),
        ),
        in_specs=[anywhere] * 3,
        out_specs=(vmem, vmem, vmem),
        scratch_shapes=[
            pltpu.VMEM(features.shape, B16),
            pltpu.VMEM((features.shape[1], lanes), F32),
            pltpu.VMEM((devices * slots, lanes), F32),
            pltpu.VMEM((hop // line, line), I32),
            pltpu.SMEM((fanout * hop,), I32),
            pltpu.SMEM((hop,), I32),
            pltpu.SemaphoreType.DMA((4,)),
            pltpu.SemaphoreType.DMA((fanout,)),
            pltpu.SemaphoreType.DMA,
            pltpu.SemaphoreType.DMA,
        ],
        cost_estimate=pl.CostEstimate(flops=4 * 10**11, bytes_accessed=10**9, transcendentals=0),
        compiler_params=pltpu.CompilerParams(vmem_limit_bytes=GATHER_VMEM),
    )(neighbors.T, targets.reshape(-1, line), features)

    x = lax.all_to_all(out, "feat", 0, 0, tiled=True)
    mine, own_tgt = lax.optimization_barrier((mine, own_tgt))
    theirs = to_core(mine)

    prepared_shapes = (
        jax.ShapeDtypeStruct((nodes, group), B16),
        jax.ShapeDtypeStruct((group, width), F32),
        jax.ShapeDtypeStruct((nodes, wide), B16),
        jax.ShapeDtypeStruct((wide, width), B16),
        jax.ShapeDtypeStruct((nodes, 1), F32),
    )
    prepared_scratch = [pltpu.VMEM(v.shape, v.dtype) for v in prepared_shapes]
    prepared = pl.pallas_call(
        prepare_kernel,
        out_shape=prepared_shapes,
        in_specs=[anywhere] * 8,
        out_specs=(anywhere,) * 5,
        scratch_shapes=[pltpu.VMEM((hop * n_dp // line, line), I32)]
        + [pltpu.VMEM((1, hop), I32)] * 2
        + [pltpu.VMEM(pair_grad.shape, B16)] * 4
        + [pltpu.VMEM((classes, width), B16)]
        + prepared_scratch
        + [pltpu.SemaphoreType.DMA((13,))],
        compiler_params=pltpu.CompilerParams(vmem_limit_bytes=WINDOW_VMEM),
    )(
        targets.reshape(-1, line),
        own_tgt,
        own_place,
        pair_grad,
        *other_grads,
        head_weight.T,
    )
    small_shape = jax.ShapeDtypeStruct((n_dp, z_rows, 2 * width + wide), B16)
    part_shape = jax.ShapeDtypeStruct((n_feat, half, width), B16)
    keep, send, small = pl.pallas_call(
        layer_kernel,
        out_shape=(part_shape, part_shape, small_shape),
        in_specs=[anywhere] * 8,
        out_specs=(anywhere,) * 3,
        scratch_shapes=[pltpu.VMEM(x.shape, B16), pltpu.VMEM(mine.shape, B16), pltpu.VMEM(theirs.shape, B16)]
        + prepared_scratch
        + [pltpu.VMEM(part_shape.shape, B16)] * 2
        + [pltpu.VMEM(small_shape.shape, B16)]
        + [pltpu.SemaphoreType.DMA((4, 3)), pltpu.SemaphoreType.DMA((6,))],
        compiler_params=params,
    )(x, mine, theirs, *prepared)
    pair_part = (keep.astype(F32) + to_core(send).astype(F32)).astype(B16)

    small = lax.all_to_all(small, "dp", 0, 0, tiled=True)
    small, pair_part = lax.optimization_barrier((small, pair_part))
    small = jnp.sum(small.astype(F32), axis=0)
    z = small[:, :width]
    rest = small[:, 2 * width :]
    rest = jnp.concatenate([rest[: z_rows // 2], rest[z_rows // 2 :]], axis=1)
    small = jnp.concatenate([small[:, width : 2 * width], rest], axis=0)
    logits = jnp.concatenate([z[:, :classes], z[:, wide : wide + classes]], axis=0).astype(B16)

    head_piece = jnp.broadcast_to(small[None].astype(B16), (n_feat, head_share, width))
    parts = lax.all_to_all(
        jnp.concatenate([pair_part, head_piece], axis=1), "feat", 0, 0, tiled=True
    )
    summed = jnp.sum(parts.astype(F32), axis=0).astype(B16)
    arrived = [to_row(summed, k) for k in (1, 2, 3)]
    grads = [values[:half].astype(F32) for values in [summed] + arrived]
    grad = ((grads[0] + grads[1]) + (grads[2] + grads[3])).astype(B16)
    heads = in_row_order(summed[half:], [values[half:] for values in arrived])
    final = jnp.concatenate([grad] + heads, axis=0)
    grad_self, grad_neigh = in_core_order(final, to_core(final))
    heads = jnp.stack(
        [v[half:].reshape(n_dp // 2, head_share, width) for v in (grad_self, grad_neigh)], axis=1
    )
    grad_head = heads.reshape(head_rows, width)[:classes].T.astype(F32)
    return logits, grad_self[:half].astype(F32), grad_neigh[:half].astype(F32), grad_head


def solution(mesh):
    return jax.shard_map(
        local,
        mesh=mesh,
        in_specs=(
            P("feat", "dp"),
            P("feat", None),
            P("feat", None),
            P(),
            P("dp", None),
            P(),
            P(("feat", "dp"), None),
        ),
        out_specs=(P(("feat", "dp"), None), P("feat", None), P("feat", None), P()),
        check_vma=False,
    )
```

```python
import functools

import jax
import jax.numpy as jnp
from jax import lax
from jax.experimental import pallas as pl
from jax.experimental.pallas import tpu as pltpu
from jax.sharding import PartitionSpec as P

B16 = jnp.bfloat16
F32 = jnp.float32
I32 = jnp.int32
ROWS = (((0,), (0,)), ((), ()))
COLS = (((1,), (1,)), ((), ()))
BATCHED = 32
VMEM_LIMIT = 60 * 1024 * 1024
GATHER_VMEM = 60 * 1024 * 1024
WINDOW_VMEM = 63 * 1024 * 1024


def dot(left, right, dims=(((1,), (0,)), ((), ()))):
    return lax.dot_general(left, right, dims, preferred_element_type=F32)


def split_two(values):
    upper = values.astype(B16)
    return upper, (values - upper.astype(F32)).astype(B16)


def gather_kernel(
    nbr, tgt, feat, out, own_tgt, place,
    held, table, rows_out, tgt_rows, ids, spots, feat_sems, nbr_sems, tgt_sem, spot_sem, *, slots, shift,
):
    half, n_cols = feat.shape
    fanout, hop = nbr.shape
    parts = feat_sems.shape[0]
    part = n_cols // parts
    chunk = 256
    line = tgt.shape[1]

    def feat_copy(p):
        at = pl.ds(p * part, part)
        return pltpu.make_async_copy(feat.at[:, at], held.at[:, at], feat_sems.at[p])

    def nbr_copy(k):
        return pltpu.make_async_copy(nbr.at[k], ids.at[pl.ds(k * hop, hop)], nbr_sems.at[k])

    lines = hop // line
    at = pl.ds(pl.multiple_of(lax.axis_index("dp") * lines, lines), lines)
    tgt_copy = pltpu.make_async_copy(tgt.at[at], tgt_rows, tgt_sem)
    tgt_copy.start()
    for p in range(parts):
        feat_copy(p).start()
    for k in range(fanout):
        nbr_copy(k).start()
    rows_out[...] = jnp.zeros_like(rows_out)
    eye = (
        lax.broadcasted_iota(I32, (chunk, chunk), 0) == lax.broadcasted_iota(I32, (chunk, chunk), 1)
    ).astype(F32).astype(B16)
    n_owners = rows_out.shape[0] // slots
    owner_ids = lax.broadcasted_iota(I32, (n_owners, line), 0)
    sample = lax.broadcasted_iota(I32, (line, 2 * line), 0)
    other = lax.broadcasted_iota(I32, (line, 2 * line), 1)
    earlier = ((sample < other) | (other >= line)).astype(F32).astype(B16)
    tgt_copy.wait()
    before = jnp.zeros((n_owners, line), F32)
    for r in range(hop // line):
        row = tgt_rows[r : r + 1, :]
        owner = lax.shift_right_logical(row, shift)
        hit = (owner_ids == owner).astype(F32)
        counted = dot(hit.astype(B16), earlier)
        rank = jnp.sum(hit * (counted[:, :line] + before), axis=0, keepdims=True)
        before = before + counted[:, line:]
        own_tgt[:, r * line : (r + 1) * line] = row
        place[:, r * line : (r + 1) * line] = owner * slots + rank.astype(I32)
    spot_copy = pltpu.make_async_copy(place.at[0], spots, spot_sem)
    spot_copy.start()

    at_once = 8

    def turn(c, _):
        for v in range(0, at_once, 2):
            at = [pl.multiple_of((c * at_once + v + i) * chunk, chunk) for i in range(2)]
            pieces = [held[:, pl.ds(a, chunk)] for a in at]
            turned = dot(eye, jnp.concatenate([pieces[0]] * 2 + [pieces[1]] * 2, axis=0), COLS)
            for i in range(2):
                table[pl.ds(at[i], chunk), :] = turned[:, 2 * half * i : 2 * half * (i + 1)]
        return 0

    steps = part // chunk // at_once
    for p in range(parts):
        feat_copy(p).wait()
        lax.fori_loop(p * steps, (p + 1) * steps, turn, 0)
    for k in range(fanout):
        nbr_copy(k).wait()
    spot_copy.wait()
    own_lane = lax.broadcasted_iota(I32, (1, 2 * half), 1) < half

    def several(j, _):
        base = j * BATCHED
        sums = []
        for u in range(BATCHED):
            rows = [table[pl.ds(ids[k * hop + base + u], 1), :] for k in range(fanout)]
            while len(rows) > 1:
                odd = rows[-1:] if len(rows) % 2 else []
                rows = [a + b for a, b in zip(rows[::2], rows[1::2])] + odd
            sums.append(jnp.where(own_lane, table[pl.ds(base + u, 1), :], rows[0]))
        for u in range(BATCHED):
            rows_out[pl.ds(spots[base + u], 1), :] = sums[u]
        return 0

    lax.fori_loop(0, hop // BATCHED, several, 0)
    scale = jnp.where(own_lane, 1.0, 1.0 / fanout)
    n_feat, deep, lanes2 = out.shape
    lanes = lanes2 // 2
    for f in range(n_feat):
        for h in range(2):
            at = (2 * f + h) * deep
            out[f, :, h * lanes : (h + 1) * lanes] = (rows_out[at : at + deep] * scale).astype(B16)


def prepare_kernel(
    tgt_any, own_tgt_any, own_place_any, pair_any, from_1_any, from_2_any, from_3_any, head_any,
    pick_any, grad_any, gl_any, wide_head_any, count_any,
    tgt, own_tgt, own_place, pair_grad, from_1, from_2, from_3, head_t, pick_t, grad_slot, gl, head, count, sems,
):
    outside = [tgt_any, own_tgt_any, own_place_any, pair_any, from_1_any, from_2_any, from_3_any, head_any]
    inside = [tgt, own_tgt, own_place, pair_grad, from_1, from_2, from_3, head_t]
    arrive = [pltpu.make_async_copy(a, b, sems.at[i]) for i, (a, b) in enumerate(zip(outside, inside))]
    outside = [pick_any, grad_any, gl_any, wide_head_any, count_any]
    inside = [pick_t, grad_slot, gl, head, count]
    leave = [pltpu.make_async_copy(a, b, sems.at[len(arrive) + i]) for i, (a, b) in enumerate(zip(inside, outside))]
    for copy in arrive:
        copy.start()
    nodes = pick_t.shape[0]
    n_slots = pick_t.shape[1]
    classes, width = head_t.shape
    feat_rank = lax.axis_index("feat")
    for copy in arrive:
        copy.wait()
    wide = gl.shape[1]
    pair = pair_grad.shape[0]
    line = tgt.shape[1]
    hop = own_tgt.shape[1]

    def ids(shape, axis):
        return lax.broadcasted_iota(I32, shape, axis)

    def ones_at(cond):
        return cond.astype(F32).astype(B16)

    digit = 16
    high, low = [], []
    for r in range(tgt.shape[0]):
        node = tgt[r : r + 1, :] - feat_rank * nodes
        high.append(ones_at(ids((digit, line), 0) == lax.shift_right_arithmetic(node, 4)))
        low.append(ones_at(ids((digit, line), 0) == lax.bitwise_and(node, digit - 1)))
    table = dot(jnp.concatenate(high, axis=1), jnp.concatenate(low, axis=1), COLS)
    of_high = ones_at(ids((nodes, digit), 1) == lax.shift_right_logical(ids((nodes, digit), 0), 4))
    of_low = (ids((nodes, digit), 1) == lax.bitwise_and(ids((nodes, digit), 0), digit - 1)).astype(F32)
    per_node = jnp.sum(dot(of_high, table.astype(B16)) * of_low, axis=1, keepdims=True)
    count[...] = jnp.maximum(per_node, 1.0)
    leave[4].start()

    node_hit = ones_at(ids((nodes, hop), 0) == own_tgt[...] - feat_rank * nodes)
    slot_hit = ones_at(ids((n_slots, hop), 0) == own_place[...] - feat_rank * n_slots)
    picked = dot(node_hit, slot_hit, COLS).astype(B16)
    pick_t[...] = picked
    leave[0].start()

    widen = ones_at(ids((classes, wide), 0) == ids((classes, wide), 1))
    for k, piece in enumerate([pair_grad, from_1, from_2, from_3]):
        at = pl.multiple_of(lax.bitwise_xor(lax.shift_right_logical(lax.axis_index("dp"), 1), k) * pair, pair)
        gl[pl.ds(at, pair), :] = dot(piece[...], widen).astype(B16)
    padded = dot(widen, head_t[...], ROWS).astype(B16)
    head[...] = padded
    leave[2].start()
    leave[3].start()
    slot_grad = dot(dot(picked, gl[...], ROWS).astype(B16), padded)
    wide_count = jnp.broadcast_to(per_node, (nodes, line)).astype(B16)
    slot_count = jnp.maximum(dot(picked, wide_count, ROWS)[:, :1], 1.0)
    grad_slot[...] = slot_grad / slot_count
    leave[1].start()
    for copy in leave:
        copy.wait()


def layer_kernel(
    x_any, mine_any, theirs_any, pick_any, grad_any, gl_any, head_any, count_any, small_any, grad_pre_any,
    x, mine, theirs, pick_t, grad_slot, gl, head, count, small, grad_pre, big_sems, sems,
):
    parts = big_sems.shape[0]
    n_feat, deep, lanes2 = x.shape
    each = n_feat // parts
    lanes = lanes2 // 2
    width = mine.shape[2]

    def big_copies(p):
        at = pl.ds(p * each, each)
        pairs = [(x_any, x), (mine_any, mine), (theirs_any, theirs)]
        return [pltpu.make_async_copy(a.at[at], b.at[at], big_sems.at[p, i]) for i, (a, b) in enumerate(pairs)]

    for p in range(parts):
        for copy in big_copies(p):
            copy.start()
    outside = [pick_any, grad_any, gl_any, head_any, count_any]
    inside = [pick_t, grad_slot, gl, head, count]
    arrive = [pltpu.make_async_copy(a, b, sems.at[i]) for i, (a, b) in enumerate(zip(outside, inside))]
    for copy in arrive:
        copy.start()
    first = lax.bitwise_and(lax.axis_index("dp"), 1) == 0

    def weights_of(f):
        a, b = mine[f], theirs[f]
        return [jnp.where(first, a, b), jnp.where(first, b, a)]

    pre = jnp.zeros((2 * deep, width), F32)
    for p in range(parts):
        for copy in big_copies(p):
            copy.wait()
        for f in range(p * each, (p + 1) * each, 2):
            pair = jnp.concatenate([rows_of(x, f), rows_of(x, f + 1)], axis=1)
            rhs = jnp.concatenate(weights_of(f) + weights_of(f + 1), axis=0)
            pre = pre + dot(pair, rhs)
    sig = jax.nn.sigmoid(pre)
    hidden = (pre * sig).astype(B16)
    for copy in arrive:
        copy.wait()
    grad_pre[...] = (grad_slot[...] * sig * (1.0 + pre * (1.0 - sig))).astype(B16)
    leave = [pltpu.make_async_copy(grad_pre, grad_pre_any, sems.at[len(arrive)])]
    leave[0].start()
    node_mean = dot(pick_t[...], hidden) / count[...]
    upper, lower = split_two(node_mean)
    part_head = dot(gl[...], upper, ROWS) + dot(gl[...], lower, ROWS)
    z = dot(upper, head[...], COLS) + dot(lower, head[...], COLS)
    groups, rows, _ = small.shape
    wide = width // 2
    for g in range(groups):
        at = 2 * rows * g
        z_part = [z[at : at + rows], z[at + rows : at + 2 * rows]]
        at = 3 * rows // 2 * g
        rest = part_head[at + rows : at + 3 * rows // 2]
        rest = jnp.concatenate([rest[:, :wide], rest[:, wide:]], axis=0)
        small[g] = jnp.concatenate(z_part + [part_head[at : at + rows], rest], axis=1).astype(B16)
    leave.append(pltpu.make_async_copy(small, small_any, sems.at[len(arrive) + 1]))
    leave[1].start()
    for copy in leave:
        copy.wait()


def rows_of(x, f):
    lanes = x.shape[2] // 2
    both = x[f]
    return jnp.concatenate([both[:, :lanes], both[:, lanes:]], axis=0)


def weight_kernel(x_any, x_sib_any, grad_any, grad_sib_any, out, x, x_sib, grads, big_sems, sems):
    parts = big_sems.shape[0]
    n_feat = x.shape[0]
    each = n_feat // parts
    slots = grad_any.shape[0]

    def x_copies(p):
        at = pl.ds(p * each, each)
        pairs = [(x_any, x), (x_sib_any, x_sib)]
        return [pltpu.make_async_copy(a.at[at], b.at[at], big_sems.at[p, i]) for i, (a, b) in enumerate(pairs)]

    grad_copies = [
        pltpu.make_async_copy(grad_any, grads.at[pl.ds(0, slots)], sems.at[0]),
        pltpu.make_async_copy(grad_sib_any, grads.at[pl.ds(slots, slots)], sems.at[1]),
    ]
    for copy in grad_copies:
        copy.start()
    for p in range(parts):
        for copy in x_copies(p):
            copy.start()
    first = lax.bitwise_and(lax.axis_index("dp"), 1) == 0
    half = out.shape[1]
    for copy in grad_copies:
        copy.wait()
    for p in range(parts):
        for copy in x_copies(p):
            copy.wait()
        for f in range(p * each, (p + 1) * each):
            both = dot(jnp.concatenate([rows_of(x, f), rows_of(x_sib, f)], axis=0), grads[...], ROWS)
            out[f] = jnp.where(first, both[:half], both[half:]).astype(B16)


def local(features, self_weight, neigh_weight, head_weight, neighbors, targets, grad_logits):
    n_feat = lax.axis_size("feat")
    n_dp = lax.axis_size("dp")
    devices = n_feat * n_dp
    hop, fanout = neighbors.shape
    half = features.shape[0]
    lanes = 2 * half
    slots = 2 * hop // devices
    batch_dev, classes = grad_logits.shape
    width = self_weight.shape[1]
    dp_rank = lax.axis_index("dp")
    feat_rank = lax.axis_index("feat")
    core = dp_rank % 2
    row = dp_rank // 2
    group = n_dp * slots
    nodes = n_dp * batch_dev
    wide = width // 2
    head_rows = 8 * n_dp * -(-classes // (8 * n_dp))
    head_share = head_rows // n_dp
    z_rows = batch_dev // 2
    assert 2 * head_share == 3 * z_rows
    vmem = pl.BlockSpec(memory_space=pltpu.VMEM)
    smem = pl.BlockSpec(memory_space=pltpu.SMEM)
    anywhere = pl.BlockSpec(memory_space=pl.ANY)
    params = pltpu.CompilerParams(vmem_limit_bytes=VMEM_LIMIT)

    def to_core(values):
        return lax.ppermute(values, "dp", [(i, i ^ 1) for i in range(n_dp)])

    def to_row(values, k):
        return lax.ppermute(values, "dp", [(i, i ^ (2 * k)) for i in range(n_dp)])

    def in_row_order(own, others):
        a = [own] + others
        a = [jnp.where(row % 2 == 1, a[i ^ 1], a[i]) for i in range(4)]
        return [jnp.where(row // 2 == 1, a[i ^ 2], a[i]) for i in range(4)]

    def in_core_order(own, other):
        return [jnp.where(core == 0, own, other), jnp.where(core == 0, other, own)]

    all_feat = (n_feat, half, width)
    mine = jnp.where(core == 0, jnp.broadcast_to(self_weight, all_feat), jnp.broadcast_to(neigh_weight, all_feat))
    mine = lax.all_to_all(mine, "feat", 0, 0, tiled=True)

    pair_grad = jnp.concatenate(in_core_order(grad_logits, to_core(grad_logits)), axis=0)
    other_grads = [to_row(pair_grad, k) for k in (1, 2, 3)]

    line = 128
    out, own_tgt, own_place = pl.pallas_call(
        functools.partial(gather_kernel, slots=slots, shift=batch_dev.bit_length() - 1),
        out_shape=(
            jax.ShapeDtypeStruct((n_feat, group // 2, 2 * lanes), B16),
            jax.ShapeDtypeStruct((1, hop), I32),
            jax.ShapeDtypeStruct((1, hop), I32),
        ),
        in_specs=[anywhere] * 3,
        out_specs=(vmem, vmem, vmem),
        scratch_shapes=[
            pltpu.VMEM(features.shape, B16),
            pltpu.VMEM((features.shape[1], lanes), F32),
            pltpu.VMEM((devices * slots, lanes), F32),
            pltpu.VMEM((hop // line, line), I32),
            pltpu.SMEM((fanout * hop,), I32),
            pltpu.SMEM((hop,), I32),
            pltpu.SemaphoreType.DMA((4,)),
            pltpu.SemaphoreType.DMA((fanout,)),
            pltpu.SemaphoreType.DMA,
            pltpu.SemaphoreType.DMA,
        ],
        cost_estimate=pl.CostEstimate(flops=4 * 10**11, bytes_accessed=10**9, transcendentals=0),
        compiler_params=pltpu.CompilerParams(vmem_limit_bytes=GATHER_VMEM),
    )(neighbors.T, targets.reshape(-1, line), features)

    x = lax.all_to_all(out, "feat", 0, 0, tiled=True)
    mine, own_tgt = lax.optimization_barrier((mine, own_tgt))
    theirs = to_core(mine)

    prepared_shapes = (
        jax.ShapeDtypeStruct((nodes, group), B16),
        jax.ShapeDtypeStruct((group, width), F32),
        jax.ShapeDtypeStruct((nodes, wide), B16),
        jax.ShapeDtypeStruct((wide, width), B16),
        jax.ShapeDtypeStruct((nodes, 1), F32),
    )
    prepared_scratch = [pltpu.VMEM(v.shape, v.dtype) for v in prepared_shapes]
    prepared = pl.pallas_call(
        prepare_kernel,
        out_shape=prepared_shapes,
        in_specs=[anywhere] * 8,
        out_specs=(anywhere,) * 5,
        scratch_shapes=[pltpu.VMEM((hop * n_dp // line, line), I32)]
        + [pltpu.VMEM((1, hop), I32)] * 2
        + [pltpu.VMEM(pair_grad.shape, B16)] * 4
        + [pltpu.VMEM((classes, width), B16)]
        + prepared_scratch
        + [pltpu.SemaphoreType.DMA((13,))],
        compiler_params=pltpu.CompilerParams(vmem_limit_bytes=WINDOW_VMEM),
    )(
        targets.reshape(-1, line),
        own_tgt,
        own_place,
        pair_grad,
        *other_grads,
        head_weight.T,
    )
    small_shape = jax.ShapeDtypeStruct((n_dp, z_rows, 2 * width + wide), B16)
    grad_shape = jax.ShapeDtypeStruct((group, width), B16)
    x, prepared = lax.optimization_barrier((x, prepared))
    x_sib = to_core(x)
    small, grad_pre = pl.pallas_call(
        layer_kernel,
        out_shape=(small_shape, grad_shape),
        in_specs=[anywhere] * 8,
        out_specs=(anywhere,) * 2,
        scratch_shapes=[pltpu.VMEM(x.shape, B16), pltpu.VMEM(mine.shape, B16), pltpu.VMEM(theirs.shape, B16)]
        + prepared_scratch
        + [pltpu.VMEM(small_shape.shape, B16), pltpu.VMEM(grad_shape.shape, B16)]
        + [pltpu.SemaphoreType.DMA((4, 3)), pltpu.SemaphoreType.DMA((7,))],
        compiler_params=params,
    )(x, mine, theirs, *prepared)
    pair_shape = jax.ShapeDtypeStruct((n_feat, half, width), B16)
    pair_part = pl.pallas_call(
        weight_kernel,
        out_shape=pair_shape,
        in_specs=[anywhere] * 4,
        out_specs=vmem,
        scratch_shapes=[
            pltpu.VMEM(x.shape, B16),
            pltpu.VMEM(x.shape, B16),
            pltpu.VMEM((2 * group, width), B16),
            pltpu.SemaphoreType.DMA((4, 2)),
            pltpu.SemaphoreType.DMA((2,)),
        ],
        cost_estimate=pl.CostEstimate(flops=10**10, bytes_accessed=3 * 10**7, transcendentals=0),
        compiler_params=pltpu.CompilerParams(vmem_limit_bytes=24 * 1024 * 1024),
    )(x, x_sib, grad_pre, to_core(grad_pre))

    small = lax.all_to_all(small, "dp", 0, 0, tiled=True)
    small, pair_part = lax.optimization_barrier((small, pair_part))
    small = jnp.sum(small.astype(F32), axis=0)
    z = small[:, :width]
    rest = small[:, 2 * width :]
    rest = jnp.concatenate([rest[: z_rows // 2], rest[z_rows // 2 :]], axis=1)
    small = jnp.concatenate([small[:, width : 2 * width], rest], axis=0)
    logits = jnp.concatenate([z[:, :classes], z[:, wide : wide + classes]], axis=0).astype(B16)

    head_piece = jnp.broadcast_to(small[None].astype(B16), (n_feat, head_share, width))
    parts = lax.all_to_all(
        jnp.concatenate([pair_part, head_piece], axis=1), "feat", 0, 0, tiled=True
    )
    summed = jnp.sum(parts.astype(F32), axis=0).astype(B16)
    arrived = [to_row(summed, k) for k in (1, 2, 3)]
    grads = [values[:half].astype(F32) for values in [summed] + arrived]
    grad = ((grads[0] + grads[1]) + (grads[2] + grads[3])).astype(B16)
    heads = in_row_order(summed[half:], [values[half:] for values in arrived])
    final = jnp.concatenate([grad] + heads, axis=0)
    grad_self, grad_neigh = in_core_order(final, to_core(final))
    heads = jnp.stack(
        [v[half:].reshape(n_dp // 2, head_share, width) for v in (grad_self, grad_neigh)], axis=1
    )
    grad_head = heads.reshape(head_rows, width)[:classes].T.astype(F32)
    return logits, grad_self[:half].astype(F32), grad_neigh[:half].astype(F32), grad_head


def solution(mesh):
    return jax.shard_map(
        local,
        mesh=mesh,
        in_specs=(
            P("feat", "dp"),
            P("feat", None),
            P("feat", None),
            P(),
            P("dp", None),
            P(),
            P(("feat", "dp"), None),
        ),
        out_specs=(P(("feat", "dp"), None), P("feat", None), P("feat", None), P()),
        check_vma=False,
    )
```

```python
import functools

import jax
import jax.numpy as jnp
from jax import lax
from jax.experimental import pallas as pl
from jax.experimental.pallas import tpu as pltpu
from jax.sharding import PartitionSpec as P

B16 = jnp.bfloat16
F32 = jnp.float32
I32 = jnp.int32
ROWS = (((0,), (0,)), ((), ()))
COLS = (((1,), (1,)), ((), ()))
BATCHED = 64
VMEM_LIMIT = 60 * 1024 * 1024
GATHER_VMEM = 60 * 1024 * 1024
WINDOW_VMEM = 63 * 1024 * 1024


def dot(left, right, dims=(((1,), (0,)), ((), ()))):
    return lax.dot_general(left, right, dims, preferred_element_type=F32)


def split_two(values):
    upper = values.astype(B16)
    return upper, (values - upper.astype(F32)).astype(B16)


def gather_kernel(
    nbr, tgt, feat, out, own_tgt, place,
    held, table, rows_out, tgt_rows, ids, spots, feat_sems, nbr_sems, tgt_sem, spot_sem, *, slots, shift,
):
    half, n_cols = feat.shape
    fanout, hop = nbr.shape
    parts = feat_sems.shape[0]
    part = n_cols // parts
    chunk = 256
    line = tgt.shape[1]

    def feat_copy(p):
        at = pl.ds(p * part, part)
        return pltpu.make_async_copy(feat.at[:, at], held.at[:, at], feat_sems.at[p])

    def nbr_copy(k):
        return pltpu.make_async_copy(nbr.at[k], ids.at[pl.ds(k * hop, hop)], nbr_sems.at[k])

    lines = hop // line
    at = pl.ds(pl.multiple_of(lax.axis_index("dp") * lines, lines), lines)
    tgt_copy = pltpu.make_async_copy(tgt.at[at], tgt_rows, tgt_sem)
    tgt_copy.start()
    for p in range(parts):
        feat_copy(p).start()
    for k in range(fanout):
        nbr_copy(k).start()
    rows_out[...] = jnp.zeros_like(rows_out)
    eye = (
        lax.broadcasted_iota(I32, (chunk, chunk), 0) == lax.broadcasted_iota(I32, (chunk, chunk), 1)
    ).astype(F32).astype(B16)
    n_owners = rows_out.shape[0] // slots
    owner_ids = lax.broadcasted_iota(I32, (n_owners, line), 0)
    sample = lax.broadcasted_iota(I32, (line, 2 * line), 0)
    other = lax.broadcasted_iota(I32, (line, 2 * line), 1)
    earlier = ((sample < other) | (other >= line)).astype(F32).astype(B16)
    tgt_copy.wait()
    before = jnp.zeros((n_owners, line), F32)
    for r in range(hop // line):
        row = tgt_rows[r : r + 1, :]
        owner = lax.shift_right_logical(row, shift)
        hit = (owner_ids == owner).astype(F32)
        counted = dot(hit.astype(B16), earlier)
        rank = jnp.sum(hit * (counted[:, :line] + before), axis=0, keepdims=True)
        before = before + counted[:, line:]
        own_tgt[:, r * line : (r + 1) * line] = row
        place[:, r * line : (r + 1) * line] = owner * slots + rank.astype(I32)
    spot_copy = pltpu.make_async_copy(place.at[0], spots, spot_sem)
    spot_copy.start()

    at_once = 8

    def turn(c, _):
        for v in range(0, at_once, 2):
            at = [pl.multiple_of((c * at_once + v + i) * chunk, chunk) for i in range(2)]
            pieces = [held[:, pl.ds(a, chunk)] for a in at]
            turned = dot(eye, jnp.concatenate([pieces[0]] * 2 + [pieces[1]] * 2, axis=0), COLS)
            for i in range(2):
                table[pl.ds(at[i], chunk), :] = turned[:, 2 * half * i : 2 * half * (i + 1)]
        return 0

    steps = part // chunk // at_once
    for p in range(parts):
        feat_copy(p).wait()
        lax.fori_loop(p * steps, (p + 1) * steps, turn, 0)
    for k in range(fanout):
        nbr_copy(k).wait()
    spot_copy.wait()
    own_lane = lax.broadcasted_iota(I32, (1, 2 * half), 1) < half

    def several(j, _):
        base = j * BATCHED
        sums = []
        for u in range(BATCHED):
            rows = [table[pl.ds(ids[k * hop + base + u], 1), :] for k in range(fanout)]
            while len(rows) > 1:
                odd = rows[-1:] if len(rows) % 2 else []
                rows = [a + b for a, b in zip(rows[::2], rows[1::2])] + odd
            sums.append(jnp.where(own_lane, table[pl.ds(base + u, 1), :], rows[0]))
        for u in range(BATCHED):
            rows_out[pl.ds(spots[base + u], 1), :] = sums[u]
        return 0

    lax.fori_loop(0, hop // BATCHED, several, 0)
    scale = jnp.where(own_lane, 1.0, 1.0 / fanout)
    n_feat, deep, lanes2 = out.shape
    lanes = lanes2 // 2
    for f in range(n_feat):
        for h in range(2):
            at = (2 * f + h) * deep
            out[f, :, h * lanes : (h + 1) * lanes] = (rows_out[at : at + deep] * scale).astype(B16)


def prepare_kernel(
    tgt_any, own_tgt_any, own_place_any, pair_any, from_1_any, from_2_any, from_3_any, head_any,
    pick_any, grad_any, gl_any, wide_head_any, count_any,
    tgt, own_tgt, own_place, pair_grad, from_1, from_2, from_3, head_t, pick_t, grad_slot, gl, head, count, sems,
):
    outside = [tgt_any, own_tgt_any, own_place_any, pair_any, from_1_any, from_2_any, from_3_any, head_any]
    inside = [tgt, own_tgt, own_place, pair_grad, from_1, from_2, from_3, head_t]
    arrive = [pltpu.make_async_copy(a, b, sems.at[i]) for i, (a, b) in enumerate(zip(outside, inside))]
    outside = [pick_any, grad_any, gl_any, wide_head_any, count_any]
    inside = [pick_t, grad_slot, gl, head, count]
    leave = [pltpu.make_async_copy(a, b, sems.at[len(arrive) + i]) for i, (a, b) in enumerate(zip(inside, outside))]
    for copy in arrive:
        copy.start()
    nodes = pick_t.shape[0]
    n_slots = pick_t.shape[1]
    classes, width = head_t.shape
    feat_rank = lax.axis_index("feat")
    for copy in arrive:
        copy.wait()
    wide = gl.shape[1]
    pair = pair_grad.shape[0]
    line = tgt.shape[1]
    hop = own_tgt.shape[1]

    def ids(shape, axis):
        return lax.broadcasted_iota(I32, shape, axis)

    def ones_at(cond):
        return cond.astype(F32).astype(B16)

    digit = 16
    high, low = [], []
    for r in range(tgt.shape[0]):
        node = tgt[r : r + 1, :] - feat_rank * nodes
        high.append(ones_at(ids((digit, line), 0) == lax.shift_right_arithmetic(node, 4)))
        low.append(ones_at(ids((digit, line), 0) == lax.bitwise_and(node, digit - 1)))
    table = dot(jnp.concatenate(high, axis=1), jnp.concatenate(low, axis=1), COLS)
    of_high = ones_at(ids((nodes, digit), 1) == lax.shift_right_logical(ids((nodes, digit), 0), 4))
    of_low = (ids((nodes, digit), 1) == lax.bitwise_and(ids((nodes, digit), 0), digit - 1)).astype(F32)
    per_node = jnp.sum(dot(of_high, table.astype(B16)) * of_low, axis=1, keepdims=True)
    count[...] = jnp.maximum(per_node, 1.0)
    leave[4].start()

    node_hit = ones_at(ids((nodes, hop), 0) == own_tgt[...] - feat_rank * nodes)
    slot_hit = ones_at(ids((n_slots, hop), 0) == own_place[...] - feat_rank * n_slots)
    picked = dot(node_hit, slot_hit, COLS).astype(B16)
    pick_t[...] = picked
    leave[0].start()

    widen = ones_at(ids((classes, wide), 0) == ids((classes, wide), 1))
    for k, piece in enumerate([pair_grad, from_1, from_2, from_3]):
        at = pl.multiple_of(lax.bitwise_xor(lax.shift_right_logical(lax.axis_index("dp"), 1), k) * pair, pair)
        gl[pl.ds(at, pair), :] = dot(piece[...], widen).astype(B16)
    padded = dot(widen, head_t[...], ROWS).astype(B16)
    head[...] = padded
    leave[2].start()
    leave[3].start()
    slot_grad = dot(dot(picked, gl[...], ROWS).astype(B16), padded)
    wide_count = jnp.broadcast_to(per_node, (nodes, line)).astype(B16)
    slot_count = jnp.maximum(dot(picked, wide_count, ROWS)[:, :1], 1.0)
    grad_slot[...] = slot_grad / slot_count
    leave[1].start()
    for copy in leave:
        copy.wait()


def layer_kernel(
    x_any, mine_any, theirs_any, pick_any, grad_any, gl_any, head_any, count_any, small_any, grad_pre_any,
    x, mine, theirs, pick_t, grad_slot, gl, head, count, small, grad_pre, big_sems, sems,
):
    parts = big_sems.shape[0]
    n_feat, deep, lanes2 = x.shape
    each = n_feat // parts
    lanes = lanes2 // 2
    width = mine.shape[2]

    def big_copies(p):
        at = pl.ds(p * each, each)
        pairs = [(x_any, x), (mine_any, mine), (theirs_any, theirs)]
        return [pltpu.make_async_copy(a.at[at], b.at[at], big_sems.at[p, i]) for i, (a, b) in enumerate(pairs)]

    for p in range(parts):
        for copy in big_copies(p):
            copy.start()
    outside = [pick_any, grad_any, gl_any, head_any, count_any]
    inside = [pick_t, grad_slot, gl, head, count]
    arrive = [pltpu.make_async_copy(a, b, sems.at[i]) for i, (a, b) in enumerate(zip(outside, inside))]
    for copy in arrive:
        copy.start()
    first = lax.bitwise_and(lax.axis_index("dp"), 1) == 0

    def weights_of(f):
        a, b = mine[f], theirs[f]
        return [jnp.where(first, a, b), jnp.where(first, b, a)]

    pre = jnp.zeros((2 * deep, width), F32)
    for p in range(parts):
        for copy in big_copies(p):
            copy.wait()
        for f in range(p * each, (p + 1) * each, 2):
            pair = jnp.concatenate([rows_of(x, f), rows_of(x, f + 1)], axis=1)
            rhs = jnp.concatenate(weights_of(f) + weights_of(f + 1), axis=0)
            pre = pre + dot(pair, rhs)
    sig = jax.nn.sigmoid(pre)
    hidden = (pre * sig).astype(B16)
    for copy in arrive:
        copy.wait()
    grad_pre[...] = (grad_slot[...] * sig * (1.0 + pre * (1.0 - sig))).astype(B16)
    leave = [pltpu.make_async_copy(grad_pre, grad_pre_any, sems.at[len(arrive)])]
    leave[0].start()
    node_mean = dot(pick_t[...], hidden) / count[...]
    upper, lower = split_two(node_mean)
    part_head = dot(gl[...], upper, ROWS) + dot(gl[...], lower, ROWS)
    z = dot(upper, head[...], COLS) + dot(lower, head[...], COLS)
    groups, rows, _ = small.shape
    wide = width // 2
    for g in range(groups):
        at = 2 * rows * g
        z_part = [z[at : at + rows], z[at + rows : at + 2 * rows]]
        at = 3 * rows // 2 * g
        rest = part_head[at + rows : at + 3 * rows // 2]
        rest = jnp.concatenate([rest[:, :wide], rest[:, wide:]], axis=0)
        small[g] = jnp.concatenate(z_part + [part_head[at : at + rows], rest], axis=1).astype(B16)
    leave.append(pltpu.make_async_copy(small, small_any, sems.at[len(arrive) + 1]))
    leave[1].start()
    for copy in leave:
        copy.wait()


def rows_of(x, f):
    lanes = x.shape[2] // 2
    both = x[f]
    return jnp.concatenate([both[:, :lanes], both[:, lanes:]], axis=0)


def weight_kernel(x_any, x_sib_any, grad_any, grad_sib_any, out, x, x_sib, grads, big_sems, sems):
    parts = big_sems.shape[0]
    n_feat = x.shape[0]
    each = n_feat // parts
    slots = grad_any.shape[0]

    def x_copies(p):
        at = pl.ds(p * each, each)
        pairs = [(x_any, x), (x_sib_any, x_sib)]
        return [pltpu.make_async_copy(a.at[at], b.at[at], big_sems.at[p, i]) for i, (a, b) in enumerate(pairs)]

    grad_copies = [
        pltpu.make_async_copy(grad_any, grads.at[pl.ds(0, slots)], sems.at[0]),
        pltpu.make_async_copy(grad_sib_any, grads.at[pl.ds(slots, slots)], sems.at[1]),
    ]
    for copy in grad_copies:
        copy.start()
    for p in range(parts):
        for copy in x_copies(p):
            copy.start()
    first = lax.bitwise_and(lax.axis_index("dp"), 1) == 0
    half = out.shape[1]
    for copy in grad_copies:
        copy.wait()
    for p in range(parts):
        for copy in x_copies(p):
            copy.wait()
        for f in range(p * each, (p + 1) * each):
            both = dot(jnp.concatenate([rows_of(x, f), rows_of(x_sib, f)], axis=0), grads[...], ROWS)
            out[f] = jnp.where(first, both[:half], both[half:]).astype(B16)


def local(features, self_weight, neigh_weight, head_weight, neighbors, targets, grad_logits):
    n_feat = lax.axis_size("feat")
    n_dp = lax.axis_size("dp")
    devices = n_feat * n_dp
    hop, fanout = neighbors.shape
    half = features.shape[0]
    lanes = 2 * half
    slots = 2 * hop // devices
    batch_dev, classes = grad_logits.shape
    width = self_weight.shape[1]
    dp_rank = lax.axis_index("dp")
    feat_rank = lax.axis_index("feat")
    core = dp_rank % 2
    row = dp_rank // 2
    group = n_dp * slots
    nodes = n_dp * batch_dev
    wide = width // 2
    head_rows = 8 * n_dp * -(-classes // (8 * n_dp))
    head_share = head_rows // n_dp
    z_rows = batch_dev // 2
    assert 2 * head_share == 3 * z_rows
    vmem = pl.BlockSpec(memory_space=pltpu.VMEM)
    smem = pl.BlockSpec(memory_space=pltpu.SMEM)
    anywhere = pl.BlockSpec(memory_space=pl.ANY)
    params = pltpu.CompilerParams(vmem_limit_bytes=VMEM_LIMIT)

    def to_core(values):
        return lax.ppermute(values, "dp", [(i, i ^ 1) for i in range(n_dp)])

    def to_row(values, k):
        return lax.ppermute(values, "dp", [(i, i ^ (2 * k)) for i in range(n_dp)])

    def in_row_order(own, others):
        a = [own] + others
        a = [jnp.where(row % 2 == 1, a[i ^ 1], a[i]) for i in range(4)]
        return [jnp.where(row // 2 == 1, a[i ^ 2], a[i]) for i in range(4)]

    def in_core_order(own, other):
        return [jnp.where(core == 0, own, other), jnp.where(core == 0, other, own)]

    all_feat = (n_feat, half, width)
    mine = jnp.where(core == 0, jnp.broadcast_to(self_weight, all_feat), jnp.broadcast_to(neigh_weight, all_feat))
    mine = lax.all_to_all(mine, "feat", 0, 0, tiled=True)

    pair_grad = jnp.concatenate(in_core_order(grad_logits, to_core(grad_logits)), axis=0)
    other_grads = [to_row(pair_grad, k) for k in (1, 2, 3)]

    line = 128
    out, own_tgt, own_place = pl.pallas_call(
        functools.partial(gather_kernel, slots=slots, shift=batch_dev.bit_length() - 1),
        out_shape=(
            jax.ShapeDtypeStruct((n_feat, group // 2, 2 * lanes), B16),
            jax.ShapeDtypeStruct((1, hop), I32),
            jax.ShapeDtypeStruct((1, hop), I32),
        ),
        in_specs=[anywhere] * 3,
        out_specs=(vmem, vmem, vmem),
        scratch_shapes=[
            pltpu.VMEM(features.shape, B16),
            pltpu.VMEM((features.shape[1], lanes), F32),
            pltpu.VMEM((devices * slots, lanes), F32),
            pltpu.VMEM((hop // line, line), I32),
            pltpu.SMEM((fanout * hop,), I32),
            pltpu.SMEM((hop,), I32),
            pltpu.SemaphoreType.DMA((4,)),
            pltpu.SemaphoreType.DMA((fanout,)),
            pltpu.SemaphoreType.DMA,
            pltpu.SemaphoreType.DMA,
        ],
        cost_estimate=pl.CostEstimate(flops=4 * 10**11, bytes_accessed=10**9, transcendentals=0),
        compiler_params=pltpu.CompilerParams(vmem_limit_bytes=GATHER_VMEM),
    )(neighbors.T, targets.reshape(-1, line), features)

    x = lax.all_to_all(out, "feat", 0, 0, tiled=True)
    mine, own_tgt = lax.optimization_barrier((mine, own_tgt))
    theirs = to_core(mine)

    prepared_shapes = (
        jax.ShapeDtypeStruct((nodes, group), B16),
        jax.ShapeDtypeStruct((group, width), F32),
        jax.ShapeDtypeStruct((nodes, wide), B16),
        jax.ShapeDtypeStruct((wide, width), B16),
        jax.ShapeDtypeStruct((nodes, 1), F32),
    )
    prepared_scratch = [pltpu.VMEM(v.shape, v.dtype) for v in prepared_shapes]
    prepared = pl.pallas_call(
        prepare_kernel,
        out_shape=prepared_shapes,
        in_specs=[anywhere] * 8,
        out_specs=(anywhere,) * 5,
        scratch_shapes=[pltpu.VMEM((hop * n_dp // line, line), I32)]
        + [pltpu.VMEM((1, hop), I32)] * 2
        + [pltpu.VMEM(pair_grad.shape, B16)] * 4
        + [pltpu.VMEM((classes, width), B16)]
        + prepared_scratch
        + [pltpu.SemaphoreType.DMA((13,))],
        compiler_params=pltpu.CompilerParams(vmem_limit_bytes=WINDOW_VMEM),
    )(
        targets.reshape(-1, line),
        own_tgt,
        own_place,
        pair_grad,
        *other_grads,
        head_weight.T,
    )
    small_shape = jax.ShapeDtypeStruct((n_dp, z_rows, 2 * width + wide), B16)
    grad_shape = jax.ShapeDtypeStruct((group, width), B16)
    x, prepared = lax.optimization_barrier((x, prepared))
    x_sib = to_core(x)
    small, grad_pre = pl.pallas_call(
        layer_kernel,
        out_shape=(small_shape, grad_shape),
        in_specs=[anywhere] * 8,
        out_specs=(anywhere,) * 2,
        scratch_shapes=[pltpu.VMEM(x.shape, B16), pltpu.VMEM(mine.shape, B16), pltpu.VMEM(theirs.shape, B16)]
        + prepared_scratch
        + [pltpu.VMEM(small_shape.shape, B16), pltpu.VMEM(grad_shape.shape, B16)]
        + [pltpu.SemaphoreType.DMA((4, 3)), pltpu.SemaphoreType.DMA((7,))],
        compiler_params=params,
    )(x, mine, theirs, *prepared)
    pair_shape = jax.ShapeDtypeStruct((n_feat, half, width), B16)
    pair_part = pl.pallas_call(
        weight_kernel,
        out_shape=pair_shape,
        in_specs=[anywhere] * 4,
        out_specs=vmem,
        scratch_shapes=[
            pltpu.VMEM(x.shape, B16),
            pltpu.VMEM(x.shape, B16),
            pltpu.VMEM((2 * group, width), B16),
            pltpu.SemaphoreType.DMA((4, 2)),
            pltpu.SemaphoreType.DMA((2,)),
        ],
        cost_estimate=pl.CostEstimate(flops=10**10, bytes_accessed=3 * 10**7, transcendentals=0),
        compiler_params=pltpu.CompilerParams(vmem_limit_bytes=24 * 1024 * 1024),
    )(x, x_sib, grad_pre, to_core(grad_pre))

    small = lax.all_to_all(small, "dp", 0, 0, tiled=True)
    small, pair_part = lax.optimization_barrier((small, pair_part))
    small = jnp.sum(small.astype(F32), axis=0)
    z = small[:, :width]
    rest = small[:, 2 * width :]
    rest = jnp.concatenate([rest[: z_rows // 2], rest[z_rows // 2 :]], axis=1)
    small = jnp.concatenate([small[:, width : 2 * width], rest], axis=0)
    logits = jnp.concatenate([z[:, :classes], z[:, wide : wide + classes]], axis=0).astype(B16)

    head_piece = jnp.broadcast_to(small[None].astype(B16), (n_feat, head_share, width))
    parts = lax.all_to_all(
        jnp.concatenate([pair_part, head_piece], axis=1), "feat", 0, 0, tiled=True
    )
    summed = jnp.sum(parts.astype(F32), axis=0).astype(B16)
    arrived = [to_row(summed, k) for k in (1, 2, 3)]
    grads = [values[:half].astype(F32) for values in [summed] + arrived]
    grad = ((grads[0] + grads[1]) + (grads[2] + grads[3])).astype(B16)
    heads = in_row_order(summed[half:], [values[half:] for values in arrived])
    final = jnp.concatenate([grad] + heads, axis=0)
    grad_self, grad_neigh = in_core_order(final, to_core(final))
    heads = jnp.stack(
        [v[half:].reshape(n_dp // 2, head_share, width) for v in (grad_self, grad_neigh)], axis=1
    )
    grad_head = heads.reshape(head_rows, width)[:classes].T.astype(F32)
    return logits, grad_self[:half].astype(F32), grad_neigh[:half].astype(F32), grad_head


def solution(mesh):
    return jax.shard_map(
        local,
        mesh=mesh,
        in_specs=(
            P("feat", "dp"),
            P("feat", None),
            P("feat", None),
            P(),
            P("dp", None),
            P(),
            P(("feat", "dp"), None),
        ),
        out_specs=(P(("feat", "dp"), None), P("feat", None), P("feat", None), P()),
        check_vma=False,
    )
```
